32 devices in a mesh: group: 16 (over z, x, core), shard: 2 (over y).
Axes of the slice: x: 2, y: 2, z: 4, core: 2. Of those that a mesh axis runs over, the one named last changes fastest.
Arguments:
- owners: int32 [6], replicated, may hold values from 0 to 1, as said below
- mat_weight: bfloat16 [6, 128, 4096], P(None, 'shard'), may hold values from -0.09375 to 0.09375
- mat_grad: bfloat16 [16, 6, 128, 4096], P('group', None, 'shard'), may hold values from -2 to 2
- head_block_momentum: bfloat16 [6, 128, 4096], P(None, 'shard'), may hold values from -48 to 48
- emb_weight: bfloat16 [64, 4096], P('shard'), may hold values from -6 to 6
- emb_grad: bfloat16 [16, 64, 4096], P('group', 'shard'), may hold values from -2 to 2
- emb_first: float32 [64, 4096], P('shard'), may hold values from -6 to 6
- emb_second: float32 [64, 4096], P('shard'), may hold values from 0.1 to 10
- norm_weight: bfloat16 [2, 4096], P(None, 'shard'), may hold values from 0.5 to 1.5
- norm_grad: bfloat16 [16, 2, 4096], P('group', None, 'shard'), may hold values from -2 to 2
- norm_first: float32 [2, 4096], P(None, 'shard'), may hold values from -6 to 6
- norm_second: float32 [2, 4096], P(None, 'shard'), may hold values from 0.1 to 10
- qk_weight: bfloat16 [2, 128], replicated, may hold values from 0.5 to 1.5
- qk_grad: bfloat16 [16, 2, 128], P('group'), may hold values from -2 to 2
- qk_first: float32 [2, 128], replicated, may hold values from -6 to 6
- qk_second: float32 [2, 128], replicated, may hold values from 0.1 to 10
Outputs:
- new_weight: bfloat16 [6, 128, 4096], P(None, 'shard')
- new_moment: bfloat16 [6, 128, 4096], P(None, 'shard')
- owner_sums: float32 [2, 3], P('shard')
- emb_new: bfloat16 [64, 4096], P('shard')
- emb_first_new: float32 [64, 4096], P('shard')
- emb_second_new: float32 [64, 4096], P('shard')
- norm_new: bfloat16 [2, 4096], P(None, 'shard')
- norm_first_new: float32 [2, 4096], P(None, 'shard')
- norm_second_new: float32 [2, 4096], P(None, 'shard')
- qk_new: bfloat16 [2, 128], replicated
- qk_first_new: float32 [2, 128], replicated
- qk_second_new: float32 [2, 128], replicated
The draws below stay inside these ranges and needn't reach their ends.
Inputs may be any that keep to these rules, and one draw needn't show every extreme that they name: `owners`: each shard rank owns at most 3 head blocks, and some rank owns exactly 3.
All inputs are finite; a program needn't handle non-finite values.
Results may differ from the reference program's by a relative error of at most 0.008.
Values may be sent and summed in bfloat16 or wider, within the bound.
A program may use at most 64 MiB of HBM per device.

```python
import math
import jax
import jax.numpy as jnp
from jax import lax

D = 4096
HEAD = 128
MATS = 6
NS_ITERS = 5
CAP = 3
EMB_ROWS = 64
N_GROUP = 16
N_SHARD = 2


def draw_owners(key, part):
    score_key = jax.random.fold_in(key, 11)
    order_key = jax.random.fold_in(key, 23)
    ranks = jnp.arange(N_SHARD, dtype=jnp.int32)
    scores = jax.random.randint(score_key, (N_SHARD,), 0, 1 << 20, dtype=jnp.int32) * N_SHARD + ranks
    scores = jnp.where(ranks == N_SHARD - 1, -2, jnp.where(ranks == 0, -1, scores))
    sequence = jnp.argsort(scores, stable=True).astype(jnp.int32)
    cyclic = sequence[jnp.arange(MATS) % N_SHARD]
    shuffled = jax.random.permutation(order_key, MATS)
    return cyclic[shuffled].astype(jnp.int32)


def draw_head_block_momentum(key, part):
    scale_key = jax.random.fold_in(key, 37)
    value_key = jax.random.fold_in(key, 41)
    spread = jax.random.uniform(scale_key, (MATS, 1, 1), jnp.float32, jnp.log(0.5), jnp.log(8.0))
    scales = jnp.exp(spread)
    values = jnp.clip(jax.random.normal(value_key, (MATS, HEAD, D), jnp.float32), -6.0, 6.0)
    return (values * scales).astype(jnp.bfloat16)


def block_scale(stream_key, dims, shards, low, top_value):
    loudness = 1.0
    for dim, shards_of in shards:
        draws = jax.random.uniform(jax.random.fold_in(jax.random.fold_in(stream_key, 6), dim), (shards_of,), jnp.float32, low / len(shards), top_value / len(shards))
        loudness = loudness * jnp.repeat(jnp.exp(draws), dims[dim] // shards_of).reshape((-1,) + (1,) * (len(dims) - 1 - dim))
    return loudness


def normal_values(own_key, extent, scale, most, split=(), kind=jnp.bfloat16):
    result = jax.random.normal(own_key, extent, jnp.float32) * scale
    if len(split) > 0:
        result = block_scale(own_key, extent, split, -0.22, 0.18) * result
    return jnp.clip(result, min=-most, max=most).astype(kind)


def setup_inputs(seed: int = 0) -> dict:
    streams_of = jax.random.split(jax.random.key(seed), 17)
    owners = draw_owners(jax.random.fold_in(streams_of[16], 71), 0)
    mat_weight = normal_values(streams_of[1], (MATS, HEAD, D), D ** -0.5, 0.09375, ((1, 2),))
    mat_grad = normal_values(streams_of[2], (N_GROUP, MATS, HEAD, D), 0.125, 2.0, ((0, 16), (2, 2)))
    head_block_momentum = draw_head_block_momentum(jax.random.fold_in(streams_of[16], 71), 0)
    emb_weight = normal_values(streams_of[4], (EMB_ROWS, D), 1.0, 6.0, ((0, 2),))
    emb_grad = normal_values(streams_of[5], (N_GROUP, EMB_ROWS, D), 0.125, 2.0, ((0, 16), (1, 2)))
    emb_first = normal_values(streams_of[6], (EMB_ROWS, D), 1.0, 6.0, ((0, 2),), jnp.float32)
    emb_second = jnp.clip(jnp.exp(math.log(10.0) - 4.6051702 * jax.random.uniform(streams_of[7], (EMB_ROWS, D), jnp.float32) ** block_scale(streams_of[7], (EMB_ROWS, D), ((0, 2),), -0.2, 0.2)), 0.1, 10.0)
    norm_weight = jnp.clip(1.0 + 0.1 * jax.random.normal(streams_of[8], (2, D), jnp.float32), 0.5, 1.5).astype(jnp.bfloat16)
    norm_grad = normal_values(streams_of[9], (N_GROUP, 2, D), 0.125, 2.0, ((0, 16), (2, 2)))
    norm_first = normal_values(streams_of[10], (2, D), 1.0, 6.0, ((1, 2),), jnp.float32)
    norm_second = jnp.clip(jnp.exp(math.log(10.0) - 4.6051702 * jax.random.uniform(streams_of[11], (2, D), jnp.float32) ** block_scale(streams_of[11], (2, D), ((1, 2),), -0.2, 0.2)), 0.1, 10.0)
    qk_weight = jnp.clip(1.0 + 0.1 * jax.random.normal(streams_of[12], (2, HEAD), jnp.float32), 0.5, 1.5).astype(jnp.bfloat16)
    qk_grad = normal_values(streams_of[13], (N_GROUP, 2, HEAD), 0.125, 2.0, ((0, 16),))
    qk_first = normal_values(streams_of[14], (2, HEAD), 1.0, 6.0, (), jnp.float32)
    qk_second = jnp.clip(jnp.exp(jax.random.uniform(streams_of[15], (2, HEAD), jnp.float32, math.log(0.1), math.log(10.0))), 0.1, 10.0)
    return dict(owners=owners, mat_weight=mat_weight, mat_grad=mat_grad, head_block_momentum=head_block_momentum, emb_weight=emb_weight, emb_grad=emb_grad, emb_first=emb_first, emb_second=emb_second, norm_weight=norm_weight, norm_grad=norm_grad, norm_first=norm_first, norm_second=norm_second, qk_weight=qk_weight, qk_grad=qk_grad, qk_first=qk_first, qk_second=qk_second)


momentum_decay = 0.95
muon_rate = 0.02
weight_decay = 0.1
adam_rate = 0.01
beta_first = 0.9
beta_second = 0.95
adam_epsilon = 1e-08
bias_first = 1.0 - 0.9 ** 10
bias_second = 1.0 - 0.95 ** 10
norm_epsilon = 1e-07
quintic_a = 3.4445
quintic_b = -4.775
quintic_c = 2.0315

def orthogonalize(matrix):
    widened = matrix.astype(jnp.float32)
    iterate = (widened / (jnp.sqrt(jnp.sum(widened * widened)) + norm_epsilon)).astype(jnp.bfloat16)
    for sweep in range(NS_ITERS):
        gram = jnp.dot(iterate, iterate.T, preferred_element_type=jnp.float32).astype(jnp.bfloat16)
        squared = jnp.dot(gram, gram, preferred_element_type=jnp.float32)
        blend = (quintic_b * gram.astype(jnp.float32) + quintic_c * squared).astype(jnp.bfloat16)
        iterate = (quintic_a * iterate.astype(jnp.float32) + jnp.dot(blend, iterate, preferred_element_type=jnp.float32)).astype(jnp.bfloat16)
    return iterate

def owner_slots(owners, capacity):
    order = jnp.arange(owners.shape[0], dtype=jnp.int32)
    same = (owners[:, None] == owners[None, :]) & (order[None, :] < order[:, None])
    position = lax.optimization_barrier(jnp.sum(same.astype(jnp.int32), axis=1))
    return owners * capacity + position

def adamw(weight, grad_sum, first, second):
    first_new = beta_first * first + (1.0 - beta_first) * grad_sum
    second_new = beta_second * second + (1.0 - beta_second) * grad_sum * grad_sum
    wide_weight = weight.astype(jnp.float32)
    stepped = first_new / bias_first / (jnp.sqrt(second_new / bias_second) + adam_epsilon) + weight_decay * wide_weight
    return ((wide_weight - adam_rate * stepped).astype(jnp.bfloat16), first_new, second_new)

def reference(owners, mat_weight, mat_grad, head_block_momentum, emb_weight, emb_grad, emb_first, emb_second, norm_weight, norm_grad, norm_first, norm_second, qk_weight, qk_grad, qk_first, qk_second):
    muon_scale = 0.2 * math.sqrt(max(HEAD, D))
    grad_total = lax.optimization_barrier(jnp.sum(mat_grad.astype(jnp.float32), axis=0))
    moment_wide = momentum_decay * head_block_momentum.astype(jnp.float32) + grad_total
    new_moment = moment_wide.astype(jnp.bfloat16)
    forwarded_rows = (grad_total + momentum_decay * moment_wide).astype(jnp.bfloat16)
    ortho = lax.map(orthogonalize, forwarded_rows)
    new_weight = (mat_weight.astype(jnp.float32) * (1.0 - muon_rate * weight_decay) - muon_rate * muon_scale * ortho.astype(jnp.float32)).astype(jnp.bfloat16)
    slots = owner_slots(owners, CAP)
    energy = lax.optimization_barrier(jnp.sum(ortho.astype(jnp.float32) * forwarded_rows.astype(jnp.float32), axis=(1, 2))) / (HEAD * math.sqrt(D))
    table = (slots[None, :] == jnp.arange(N_SHARD * CAP, dtype=jnp.int32)[:, None]).astype(jnp.float32)
    owner_sums = lax.optimization_barrier(jnp.sum(table * energy[None, :], axis=1)).reshape(N_SHARD, CAP)
    emb_new, emb_first_new, emb_second_new = adamw(emb_weight, lax.optimization_barrier(jnp.sum(emb_grad.astype(jnp.float32), axis=0)), emb_first, emb_second)
    norm_new, norm_first_new, norm_second_new = adamw(norm_weight, lax.optimization_barrier(jnp.sum(norm_grad.astype(jnp.float32), axis=0)), norm_first, norm_second)
    qk_new, qk_first_new, qk_second_new = adamw(qk_weight, lax.optimization_barrier(jnp.sum(qk_grad.astype(jnp.float32), axis=0)), qk_first, qk_second)
    return (new_weight, new_moment, owner_sums, emb_new, emb_first_new, emb_second_new, norm_new, norm_first_new, norm_second_new, qk_new, qk_first_new, qk_second_new)
```

```python
import functools
import math

import jax
import jax.numpy as jnp
from jax import lax
from jax.experimental import pallas as pl
from jax.experimental.pallas import tpu as pltpu
from jax.sharding import PartitionSpec as P

D = 4096
HEAD = 128
MATS = 6
NS_ITERS = 5


momentum_decay = 0.95
muon_rate = 0.02
weight_decay = 0.1
adam_rate = 0.01
beta_first = 0.9
beta_second = 0.95
adam_epsilon = 1e-08
bias_first = 1.0 - 0.9**10
bias_second = 1.0 - 0.95**10
norm_epsilon = 1e-07
quintic_a = 3.4445
quintic_b = -4.775
quintic_c = 2.0315


def orthogonalize(matrix):
    widened = matrix.astype(jnp.float32)
    iterate = (widened / (jnp.sqrt(jnp.sum(widened * widened)) + norm_epsilon)).astype(jnp.bfloat16)
    for sweep in range(NS_ITERS):
        gram = jnp.dot(iterate, iterate.T, preferred_element_type=jnp.float32).astype(jnp.bfloat16)
        squared = jnp.dot(gram, gram, preferred_element_type=jnp.float32)
        blend = (quintic_b * gram.astype(jnp.float32) + quintic_c * squared).astype(jnp.bfloat16)
        iterate = (
            quintic_a * iterate.astype(jnp.float32)
            + jnp.dot(blend, iterate, preferred_element_type=jnp.float32)
        ).astype(jnp.bfloat16)
    return iterate


def slot_energy(ortho, pushed):
    return jnp.sum(ortho.astype(jnp.float32) * pushed.astype(jnp.float32), axis=(1, 2)) / (
        HEAD * math.sqrt(D)
    )


def owner_slots(owners, capacity):
    order = jnp.arange(owners.shape[0], dtype=jnp.int32)
    same = (owners[:, None] == owners[None, :]) & (order[None, :] < order[:, None])
    position = jnp.sum(same.astype(jnp.int32), axis=1)
    return owners * capacity + position


def adamw(weight, grad_sum, first, second):
    first_new = beta_first * first + (1.0 - beta_first) * grad_sum
    second_new = beta_second * second + (1.0 - beta_second) * grad_sum * grad_sum
    wide_weight = weight.astype(jnp.float32)
    stepped = (
        first_new / bias_first / (jnp.sqrt(second_new / bias_second) + adam_epsilon)
        + weight_decay * wide_weight
    )
    return ((wide_weight - adam_rate * stepped).astype(jnp.bfloat16), first_new, second_new)


def on_device(
    owners,
    mat_weight,
    mat_grad,
    head_block_momentum,
    emb_weight,
    emb_grad,
    emb_first,
    emb_second,
    norm_weight,
    norm_grad,
    norm_first,
    norm_second,
    qk_weight,
    qk_grad,
    qk_first,
    qk_second,
):
    shards = lax.axis_size("shard")
    capacity = -(-MATS // shards)
    rows = mat_weight.shape[1]
    width = mat_weight.shape[2]
    muon_scale = 0.2 * math.sqrt(max(HEAD, D))
    local_grad = mat_grad[0].astype(jnp.float32)
    grad_total, emb_total, norm_total, qk_total = lax.psum(
        (
            local_grad,
            emb_grad[0].astype(jnp.float32),
            norm_grad[0].astype(jnp.float32),
            qk_grad[0].astype(jnp.float32),
        ),
        "group",
    )
    moment_wide = momentum_decay * head_block_momentum.astype(jnp.float32) + grad_total
    new_moment = moment_wide.astype(jnp.bfloat16)
    forwarded_rows = (grad_total + momentum_decay * moment_wide).astype(jnp.bfloat16)
    slots = owner_slots(owners, capacity)
    places = jnp.arange(shards * capacity, dtype=jnp.int32)
    gather_rows_back = (slots[:, None] == places[None, :]).astype(jnp.bfloat16)
    outgoing = jnp.einsum(
        "of,oyq->fyq", gather_rows_back, forwarded_rows, preferred_element_type=jnp.float32
    ).astype(jnp.bfloat16)
    outgoing = outgoing.reshape(shards, capacity, rows, width)
    items = lax.all_to_all(outgoing, "shard", split_axis=0, concat_axis=2, tiled=True)
    ortho = lax.map(orthogonalize, items[0])
    returned = lax.all_to_all(ortho[None], "shard", split_axis=2, concat_axis=0, tiled=True)
    returned, owner_sums = (returned, slot_energy(ortho, items[0])[None])
    kept_row_block = returned.reshape(shards * capacity, rows, width)
    muon_update = jnp.einsum(
        "ar,rpx->apx", gather_rows_back, kept_row_block, preferred_element_type=jnp.float32
    )
    new_weight = (
        mat_weight.astype(jnp.float32) * (1.0 - muon_rate * weight_decay)
        - muon_rate * muon_scale * muon_update
    ).astype(jnp.bfloat16)
    emb_new, emb_first_new, emb_second_new = adamw(emb_weight, emb_total, emb_first, emb_second)
    norm_new, norm_first_new, norm_second_new = adamw(
        norm_weight, norm_total, norm_first, norm_second
    )
    qk_new, qk_first_new, qk_second_new = adamw(qk_weight, qk_total, qk_first, qk_second)
    return (
        new_weight,
        new_moment,
        owner_sums,
        emb_new,
        emb_first_new,
        emb_second_new,
        norm_new,
        norm_first_new,
        norm_second_new,
        qk_new,
        qk_first_new,
        qk_second_new,
    )


SMALL_ROWS = 48
HALF_MATS = -(-MATS // 2)
TILE = 512


def links_fit(groups, shards):
    return groups & (groups - 1) == 0 and 4 <= groups <= 16 and shards == 2


def wide(value):
    return value.astype(jnp.float32)


def linked_kernel(
    bits,
    grad_ref,
    small_ref,
    moment_hbm,
    weight_hbm,
    new_weight_hbm,
    new_moment_hbm,
    small_out,
    energy_out,
    moment,
    weight,
    total,
    pushed,
    gram0,
    polynomial,
    local_sem,
    send_sem,
    recv_sem,
    *levels,
):
    landed, summed = levels[:bits], levels[bits:]
    width = grad_ref.shape[2]
    rows = grad_ref.shape[1]
    chains = MATS + 1
    widths = [width >> (level + 1) for level in range(bits)]
    me = lax.axis_index("group")
    shard = lax.axis_index("shard")
    digit = [lax.rem(lax.div(me, 1 << b), 2) for b in range(bits)]
    partner = [me + (1 << b) * (1 - 2 * digit[b]) for b in range(bits)]
    other_shard = 1 - shard

    plain = list(range(bits))
    crossed = plain if bits < 3 else [0, 2, 1] + plain[3:]
    orders = [crossed if c in (2, MATS) else plain for c in range(chains)]

    def offset(c, level):
        start = 0
        for step in range(level + 1):
            start = start + digit[orders[c][step]] * widths[step]
        return pl.multiple_of(start, widths[-1])

    barrier = pltpu.get_barrier_semaphore()
    for b in range(bits):
        pl.semaphore_signal(
            barrier, inc=1, device_id=(partner[b], shard), device_id_type=pl.DeviceIdType.MESH
        )
    pl.semaphore_signal(
        barrier, inc=1, device_id=(me, other_shard), device_id_type=pl.DeviceIdType.MESH
    )
    loads = [
        pltpu.make_async_copy(moment_hbm, moment, local_sem.at[0]),
        pltpu.make_async_copy(weight_hbm, weight, local_sem.at[1]),
    ]
    for load in loads:
        load.start()
    pl.semaphore_wait(barrier, bits + 1)

    started = {}

    def send(key, src, dst, device):
        c, slot = key
        copy = pltpu.make_async_remote_copy(
            src_ref=src,
            dst_ref=dst,
            send_sem=send_sem.at[c, slot],
            recv_sem=recv_sem.at[c, slot],
            device_id=device,
            device_id_type=pl.DeviceIdType.MESH,
        )
        copy.start()
        started[key] = copy

    def height(c):
        return rows if c < MATS else SMALL_ROWS

    def held(c, level):
        if level >= 0:
            return summed[level].at[c, pl.ds(0, height(c))]
        return grad_ref.at[c] if c < MATS else small_ref

    def scatter_start(c, level):
        b = orders[c][level]
        start = pl.multiple_of((1 - digit[b]) * widths[level], widths[level])
        send(
            (c, level),
            held(c, level - 1).at[:, pl.ds(start, widths[level])],
            landed[level].at[c, pl.ds(0, height(c))],
            (partner[b], shard),
        )

    def scatter_finish(c, level):
        started[(c, level)].wait_recv()
        b = orders[c][level]
        keep = digit[b] * widths[level]
        tile = min(TILE, widths[level])
        arrived = landed[level].at[c, pl.ds(0, height(c))]
        mine = held(c, level - 1)
        last = level == bits - 1
        place = offset(c, level) if last else 0
        target = total.at[c, pl.ds(0, height(c))] if last else held(c, level)

        def add(i, carry):
            at = pl.multiple_of(i * tile, tile)
            value = wide(arrived[:, pl.ds(at, tile)]) + wide(
                mine[:, pl.ds(pl.multiple_of(keep + at, tile), tile)]
            )
            target[:, pl.ds(pl.multiple_of(place + at, tile), tile)] = value.astype(jnp.bfloat16)
            return carry

        lax.fori_loop(0, widths[level] // tile, add, 0)

    def gather_start(c, level):
        region = total.at[c, pl.ds(0, height(c)), pl.ds(offset(c, level), widths[level])]
        send((c, bits + level), region, region, (partner[orders[c][level]], shard))

    def push(c, start):
        def step(i, carry):
            cols = pl.ds(pl.multiple_of(start + i * TILE, TILE), TILE)
            grad = wide(total[c, :, cols])
            moment_wide = momentum_decay * wide(moment[c, :, cols]) + grad
            moment[c, :, cols] = moment_wide.astype(jnp.bfloat16)
            pushed[c, 0:rows, cols] = (grad + momentum_decay * moment_wide).astype(jnp.bfloat16)
            return carry

        lax.fori_loop(0, widths[0] // TILE, step, 0)

    stores = []
    loaded = []

    def stage(c, s):
        if s == 0:
            scatter_start(c, 0)
        elif s < bits:
            scatter_finish(c, s - 1)
            scatter_start(c, s)
        elif s == bits:
            scatter_finish(c, bits - 1)
            gather_start(c, bits - 1)
        elif s < 2 * bits:
            level = 2 * bits - s
            started[(c, bits + level)].wait_recv()
            gather_start(c, level - 1)
            if level == 1 and c < MATS:
                if not loaded:
                    loads[0].wait()
                    loaded.append(0)
                push(c, offset(c, 0))
                region = pl.ds(offset(c, 0), widths[0])
                send(
                    (c, 2 * bits),
                    pushed.at[c, pl.ds(0, rows), region],
                    pushed.at[c, pl.ds(rows, rows), region],
                    (me, other_shard),
                )
        elif s == 2 * bits:
            started[(c, bits)].wait_recv()
            if c < MATS:
                push(c, widths[0] - offset(c, 0))
                store = pltpu.make_async_copy(
                    moment.at[c], new_moment_hbm.at[c], local_sem.at[2 + c]
                )
                store.start()
                stores.append(store)
            else:
                small_out[...] = total[c, 0:SMALL_ROWS]
        elif s == 2 * bits + 1:
            if c < MATS:
                started[(c, 2 * bits)].wait_recv()
                region = pushed.at[c, pl.ds(rows, rows), pl.ds(offset(c, 0), widths[0])]
                send((c, 2 * bits + 1), region, region, (partner[orders[c][0]], shard))
        elif s == 2 * bits + 2:
            if c < MATS:
                started[(c, 2 * bits + 1)].wait_recv()
                block = pushed[c]
                gram0[c] = lax.dot_general(
                    block, block, (((1,), (1,)), ((), ())), preferred_element_type=jnp.float32
                )

    stages = 2 * bits + 3
    for c in range(chains):
        stage(c, 0)
    for tick in range(1, stages + chains):
        for c in range(chains):
            s = tick - c
            if 1 <= s < stages:
                stage(c, s)

    def narrow_dot(left, right):
        return jnp.dot(
            left.astype(jnp.bfloat16),
            right.astype(jnp.bfloat16),
            preferred_element_type=jnp.float32,
        )

    here = lax.broadcasted_iota(jnp.int32, (HEAD, HEAD), 0)
    there = lax.broadcasted_iota(jnp.int32, (HEAD, HEAD), 1)
    eye = jnp.where(here == there, 1.0, 0.0).astype(jnp.float32)
    scales, grams, products = [], [], []
    for c in range(MATS):
        raw = gram0[c]
        square = jnp.sum(jnp.sum(raw * eye, axis=1, keepdims=True), axis=0, keepdims=True)
        scale = 1.0 / (jnp.sqrt(square) + norm_epsilon)
        scales.append(scale)
        grams.append(raw * scale * scale)
        products.append(None)
    for sweep in range(NS_ITERS):
        squares = [narrow_dot(g, g) for g in grams]
        blends = [
            quintic_a * eye + quintic_b * g + quintic_c * s for g, s in zip(grams, squares)
        ]
        products = [
            b if p is None else narrow_dot(b, p) for b, p in zip(blends, products)
        ]
        if sweep < NS_ITERS - 1:
            halves = [narrow_dot(b, g) for b, g in zip(blends, grams)]
            grams = [narrow_dot(h, b) for h, b in zip(halves, blends)]
    for c in range(MATS):
        scaled = products[c] * scales[c]
        energy = jnp.sum(
            jnp.sum(scaled * gram0[c], axis=1, keepdims=True), axis=0, keepdims=True
        ) / (HEAD * math.sqrt(D))
        energy_out[pl.ds(c, 1), :] = jnp.broadcast_to(energy, (1, 128))
        polynomial[c] = scaled[0:rows].astype(jnp.bfloat16)

    loads[1].wait()
    muon_scale = 0.2 * math.sqrt(max(HEAD, D))
    for c in range(MATS):

        def update(i, carry):
            cols = pl.ds(pl.multiple_of(i * TILE, TILE), TILE)
            ortho = jnp.dot(
                polynomial[c], pushed[c, :, cols], preferred_element_type=jnp.float32
            ).astype(jnp.bfloat16)
            weight[c, :, cols] = (
                wide(weight[c, :, cols]) * (1.0 - muon_rate * weight_decay)
                - muon_rate * muon_scale * wide(ortho)
            ).astype(jnp.bfloat16)
            return carry

        lax.fori_loop(0, width // TILE, update, 0)
        store = pltpu.make_async_copy(
            weight.at[c], new_weight_hbm.at[c], local_sem.at[2 + MATS + c]
        )
        store.start()
        stores.append(store)
    for copy in started.values():
        copy.wait_send()
    for store in stores:
        store.wait()


def linked_device(
    groups,
    owners,
    mat_weight,
    mat_grad,
    head_block_momentum,
    emb_weight,
    emb_grad,
    emb_first,
    emb_second,
    norm_weight,
    norm_grad,
    norm_first,
    norm_second,
    qk_weight,
    qk_grad,
    qk_first,
    qk_second,
):
    bits = groups.bit_length() - 1
    blocks, rows, width = mat_weight.shape
    emb_rows = emb_weight.shape[0]
    gains = norm_weight.shape[1]
    heads = qk_weight.shape[1]
    extra = jnp.concatenate([norm_grad[0], qk_grad[0]], axis=1)
    extra = jnp.pad(extra, ((0, SMALL_ROWS - emb_rows - 2), (0, width - gains - heads)))
    small = jnp.concatenate([emb_grad[0], extra], axis=0)
    levels = [width >> (level + 1) for level in range(bits)]
    in_vmem = pl.BlockSpec(memory_space=pltpu.VMEM)
    anywhere = pl.BlockSpec(memory_space=pl.ANY)
    block_shape = (blocks, rows, width)
    new_weight, new_moment, small_sum, energy = pl.pallas_call(
        functools.partial(linked_kernel, bits),
        out_shape=(
            jax.ShapeDtypeStruct(block_shape, jnp.bfloat16),
            jax.ShapeDtypeStruct(block_shape, jnp.bfloat16),
            jax.ShapeDtypeStruct((SMALL_ROWS, width), jnp.bfloat16),
            jax.ShapeDtypeStruct((8, 128), jnp.float32),
        ),
        in_specs=[in_vmem, in_vmem, anywhere, anywhere],
        out_specs=(anywhere, anywhere, in_vmem, in_vmem),
        scratch_shapes=[
            pltpu.VMEM(block_shape, jnp.bfloat16),
            pltpu.VMEM(block_shape, jnp.bfloat16),
            pltpu.VMEM((blocks + 1, rows, width), jnp.bfloat16),
            pltpu.VMEM((blocks, 2 * rows, width), jnp.bfloat16),
            pltpu.VMEM((blocks, HEAD, HEAD), jnp.float32),
            pltpu.VMEM((blocks, rows, HEAD), jnp.bfloat16),
            pltpu.SemaphoreType.DMA((2 + 2 * blocks,)),
            pltpu.SemaphoreType.DMA((blocks + 1, 2 * bits + 2)),
            pltpu.SemaphoreType.DMA((blocks + 1, 2 * bits + 2)),
        ]
        + [pltpu.VMEM((blocks + 1, rows, part), jnp.bfloat16) for part in levels]
        + [pltpu.VMEM((blocks + 1, rows, part), jnp.bfloat16) for part in levels[:-1]],
        compiler_params=pltpu.CompilerParams(
            collective_id=0, has_side_effects=True, vmem_limit_bytes=56 * 1024 * 1024
        ),
    )(mat_grad[0], small, head_block_momentum, mat_weight)
    small_sum = small_sum.astype(jnp.float32)
    emb_total = small_sum[:emb_rows]
    norm_total = small_sum[emb_rows : emb_rows + 2, :gains]
    qk_total = small_sum[emb_rows : emb_rows + 2, gains : gains + heads]
    slots = owner_slots(owners, HALF_MATS)
    mine = lax.axis_index("shard") * HALF_MATS + jnp.arange(HALF_MATS, dtype=jnp.int32)
    owner_sums = jnp.sum(
        jnp.where(slots[None, :] == mine[:, None], energy[:blocks, 0][None, :], 0.0), axis=1
    )[None]
    return (
        new_weight,
        new_moment,
        owner_sums,
        *adamw(emb_weight, emb_total, emb_first, emb_second),
        *adamw(norm_weight, norm_total, norm_first, norm_second),
        *adamw(qk_weight, qk_total, qk_first, qk_second),
    )


def solution(mesh):
    plan = on_device
    if links_fit(mesh.shape["group"], mesh.shape["shard"]):
        plan = functools.partial(linked_device, mesh.shape["group"])
    placed = (
        P(),
        P(None, "shard", None),
        P("group", None, "shard", None),
        P(None, "shard", None),
        P("shard", None),
        P("group", "shard", None),
        P("shard", None),
        P("shard", None),
        P(None, "shard"),
        P("group", None, "shard"),
        P(None, "shard"),
        P(None, "shard"),
        P(),
        P("group", None, None),
        P(),
        P(),
    )
    return jax.shard_map(
        plan,
        mesh=mesh,
        in_specs=placed,
        out_specs=(
            P(None, "shard", None),
            P(None, "shard", None),
            P("shard", None),
            P("shard", None),
            P("shard", None),
            P("shard", None),
            P(None, "shard"),
            P(None, "shard"),
            P(None, "shard"),
            P(),
            P(),
            P(),
        ),
        check_vma=False,
    )
```

```python
import functools
import math

import jax
import jax.numpy as jnp
from jax import lax
from jax.experimental import pallas as pl
from jax.experimental.pallas import tpu as pltpu
from jax.sharding import PartitionSpec as P

D = 4096
HEAD = 128
MATS = 6
NS_ITERS = 5


momentum_decay = 0.95
muon_rate = 0.02
weight_decay = 0.1
adam_rate = 0.01
beta_first = 0.9
beta_second = 0.95
adam_epsilon = 1e-08
bias_first = 1.0 - 0.9**10
bias_second = 1.0 - 0.95**10
norm_epsilon = 1e-07
quintic_a = 3.4445
quintic_b = -4.775
quintic_c = 2.0315


def orthogonalize(matrix):
    widened = matrix.astype(jnp.float32)
    iterate = (widened / (jnp.sqrt(jnp.sum(widened * widened)) + norm_epsilon)).astype(jnp.bfloat16)
    for sweep in range(NS_ITERS):
        gram = jnp.dot(iterate, iterate.T, preferred_element_type=jnp.float32).astype(jnp.bfloat16)
        squared = jnp.dot(gram, gram, preferred_element_type=jnp.float32)
        blend = (quintic_b * gram.astype(jnp.float32) + quintic_c * squared).astype(jnp.bfloat16)
        iterate = (
            quintic_a * iterate.astype(jnp.float32)
            + jnp.dot(blend, iterate, preferred_element_type=jnp.float32)
        ).astype(jnp.bfloat16)
    return iterate


def slot_energy(ortho, pushed):
    return jnp.sum(ortho.astype(jnp.float32) * pushed.astype(jnp.float32), axis=(1, 2)) / (
        HEAD * math.sqrt(D)
    )


def owner_slots(owners, capacity):
    order = jnp.arange(owners.shape[0], dtype=jnp.int32)
    same = (owners[:, None] == owners[None, :]) & (order[None, :] < order[:, None])
    position = jnp.sum(same.astype(jnp.int32), axis=1)
    return owners * capacity + position


def adamw(weight, grad_sum, first, second):
    first_new = beta_first * first + (1.0 - beta_first) * grad_sum
    second_new = beta_second * second + (1.0 - beta_second) * grad_sum * grad_sum
    wide_weight = weight.astype(jnp.float32)
    stepped = (
        first_new / bias_first / (jnp.sqrt(second_new / bias_second) + adam_epsilon)
        + weight_decay * wide_weight
    )
    return ((wide_weight - adam_rate * stepped).astype(jnp.bfloat16), first_new, second_new)


def on_device(
    owners,
    mat_weight,
    mat_grad,
    head_block_momentum,
    emb_weight,
    emb_grad,
    emb_first,
    emb_second,
    norm_weight,
    norm_grad,
    norm_first,
    norm_second,
    qk_weight,
    qk_grad,
    qk_first,
    qk_second,
):
    shards = lax.axis_size("shard")
    capacity = -(-MATS // shards)
    rows = mat_weight.shape[1]
    width = mat_weight.shape[2]
    muon_scale = 0.2 * math.sqrt(max(HEAD, D))
    local_grad = mat_grad[0].astype(jnp.float32)
    grad_total, emb_total, norm_total, qk_total = lax.psum(
        (
            local_grad,
            emb_grad[0].astype(jnp.float32),
            norm_grad[0].astype(jnp.float32),
            qk_grad[0].astype(jnp.float32),
        ),
        "group",
    )
    moment_wide = momentum_decay * head_block_momentum.astype(jnp.float32) + grad_total
    new_moment = moment_wide.astype(jnp.bfloat16)
    forwarded_rows = (grad_total + momentum_decay * moment_wide).astype(jnp.bfloat16)
    slots = owner_slots(owners, capacity)
    places = jnp.arange(shards * capacity, dtype=jnp.int32)
    gather_rows_back = (slots[:, None] == places[None, :]).astype(jnp.bfloat16)
    outgoing = jnp.einsum(
        "of,oyq->fyq", gather_rows_back, forwarded_rows, preferred_element_type=jnp.float32
    ).astype(jnp.bfloat16)
    outgoing = outgoing.reshape(shards, capacity, rows, width)
    items = lax.all_to_all(outgoing, "shard", split_axis=0, concat_axis=2, tiled=True)
    ortho = lax.map(orthogonalize, items[0])
    returned = lax.all_to_all(ortho[None], "shard", split_axis=2, concat_axis=0, tiled=True)
    returned, owner_sums = (returned, slot_energy(ortho, items[0])[None])
    kept_row_block = returned.reshape(shards * capacity, rows, width)
    muon_update = jnp.einsum(
        "ar,rpx->apx", gather_rows_back, kept_row_block, preferred_element_type=jnp.float32
    )
    new_weight = (
        mat_weight.astype(jnp.float32) * (1.0 - muon_rate * weight_decay)
        - muon_rate * muon_scale * muon_update
    ).astype(jnp.bfloat16)
    emb_new, emb_first_new, emb_second_new = adamw(emb_weight, emb_total, emb_first, emb_second)
    norm_new, norm_first_new, norm_second_new = adamw(
        norm_weight, norm_total, norm_first, norm_second
    )
    qk_new, qk_first_new, qk_second_new = adamw(qk_weight, qk_total, qk_first, qk_second)
    return (
        new_weight,
        new_moment,
        owner_sums,
        emb_new,
        emb_first_new,
        emb_second_new,
        norm_new,
        norm_first_new,
        norm_second_new,
        qk_new,
        qk_first_new,
        qk_second_new,
    )


SMALL_ROWS = 48
HALF_MATS = -(-MATS // 2)
TILE = 512
PIECES = 2
ORDER = (
    0, 1, 2, 3, 4, 5, 6, 7, 8, 9, 10, 11, 12, 13, 0, 1, 2, 3, 4, 5, 6, 7, 0, 8, 9, 1, 10, 11,
    2, 0, 12, 13, 1, 3, 2, 4, 0, 1, 5, 3, 2, 6, 4, 0, 7, 1, 5, 3, 8, 2, 6, 9, 4, 0, 10, 7, 1,
    11, 5, 3, 12, 8, 13, 2, 6, 0, 9, 4, 1, 10, 0, 7, 2, 5, 11, 1, 3, 12, 14, 2, 8, 13, 6, 9,
    14, 3, 15, 4, 10, 7, 5, 3, 15, 16, 8, 11, 4, 12, 13, 6, 5, 16, 17, 4, 7, 9, 10, 5, 6, 8,
    11, 17, 18, 12, 13, 9, 7, 6, 10, 11, 18, 8, 19, 7, 9, 12, 13, 8, 10, 19, 20, 11, 9, 10,
    12, 28, 13, 20, 21, 11, 12, 28, 22, 13, 21, 28, 28, 22, 23, 28, 28, 28, 23, 24, 28, 25,
    24, 25, 29, 29, 29, 29, 29, 29, 29, 29,
)


def links_fit(groups, shards):
    return groups == 16 and shards == 2


def wide(value):
    return value.astype(jnp.float32)


def linked_kernel(
    bits,
    norm_ref,
    qk_ref,
    grad_hbm,
    emb_hbm,
    moment_hbm,
    weight_hbm,
    new_weight_hbm,
    new_moment_hbm,
    small_out,
    energy_out,
    grad,
    moment,
    weight,
    small,
    total,
    pushed,
    gram0,
    gram,
    product,
    polynomial,
    local_sem,
    send_sem,
    recv_sem,
    *levels,
):
    landed, summed = levels[:bits], levels[bits:]
    rows, width = grad.shape[1], grad.shape[2] // PIECES
    chains = (MATS + 1) * PIECES
    widths = [width >> (level + 1) for level in range(bits)]
    me = lax.axis_index("group")
    shard = lax.axis_index("shard")
    digit = [lax.rem(lax.div(me, 1 << b), 2) for b in range(bits)]
    partner = [me + (1 << b) * (1 - 2 * digit[b]) for b in range(bits)]
    other_shard = 1 - shard
    offsets = []
    for level in range(bits):
        before = offsets[-1] if offsets else 0
        offsets.append(before + digit[level] * widths[level])

    barrier = pltpu.get_barrier_semaphore()
    for b in range(bits):
        pl.semaphore_signal(
            barrier, inc=1, device_id=(partner[b], shard), device_id_type=pl.DeviceIdType.MESH
        )
    pl.semaphore_signal(
        barrier, inc=1, device_id=(me, other_shard), device_id_type=pl.DeviceIdType.MESH
    )
    loads = {("grad", b): pltpu.make_async_copy(
        grad_hbm.at[b], grad.at[b], local_sem.at[3 + b]) for b in range(MATS)}
    loads["small"] = pltpu.make_async_copy(
        emb_hbm, small.at[pl.ds(0, emb_hbm.shape[0])], local_sem.at[0])
    loads["moment"] = pltpu.make_async_copy(moment_hbm, moment, local_sem.at[1])
    loads["weight"] = pltpu.make_async_copy(weight_hbm, weight, local_sem.at[2])
    for load in loads.values():
        load.start()
    extra = SMALL_ROWS - emb_hbm.shape[0]
    small[pl.ds(emb_hbm.shape[0], extra), :] = jnp.zeros((extra, small.shape[1]), jnp.bfloat16)
    place = 0
    for part in (norm_ref, qk_ref):
        tall = jnp.concatenate(
            [wide(part[...]), jnp.zeros((extra - 2, part.shape[1]), jnp.float32)], axis=0
        )
        small[pl.ds(emb_hbm.shape[0], extra), pl.ds(place, part.shape[1])] = tall.astype(
            jnp.bfloat16
        )
        place += part.shape[1]
    pl.semaphore_wait(barrier, bits + 1)

    def ready(key):
        if key in loads:
            loads.pop(key).wait()

    started = {}

    def send(c, slot, src, dst, device):
        copy = pltpu.make_async_remote_copy(
            src_ref=src,
            dst_ref=dst,
            send_sem=send_sem.at[c, slot],
            recv_sem=recv_sem.at[c, slot],
            device_id=device,
            device_id_type=pl.DeviceIdType.MESH,
        )
        copy.start()
        started[(c, slot)] = copy

    def block_of(c):
        return c // PIECES, (c % PIECES) * width

    def height(c):
        return rows if c < MATS * PIECES else SMALL_ROWS

    def held(c, level, own):
        block, base = block_of(c)
        if level >= 0:
            return summed[level].at[c, pl.ds(0, height(c))], 0
        if block == MATS:
            return small, base
        return (grad if own else grad_hbm).at[block], base

    def at_multiple(value, step):
        return value if isinstance(value, int) else pl.multiple_of(value, step)

    def scatter_start(c, level):
        if block_of(c)[0] == MATS:
            ready("small")
        source, base = held(c, level - 1, False)
        start = at_multiple(base + (1 - digit[level]) * widths[level], widths[level])
        send(
            c,
            level,
            source.at[:, pl.ds(start, widths[level])],
            landed[level].at[c, pl.ds(0, height(c))],
            (partner[level], shard),
        )

    def scatter_finish(c, level):
        block, base = block_of(c)
        if level == 0:
            ready(("grad", block))
        started[(c, level)].wait_recv()
        mine, keep = held(c, level - 1, True)
        keep = keep + digit[level] * widths[level]
        tile = min(TILE, widths[level])
        arrived = landed[level].at[c, pl.ds(0, height(c))]
        if level == bits - 1:
            target, place = total.at[block, pl.ds(0, height(c))], base + offsets[level]
        else:
            target, place = summed[level].at[c, pl.ds(0, height(c))], 0

        def add(i, carry):
            at = at_multiple(i * tile, tile)
            value = wide(arrived[:, pl.ds(at, tile)]) + wide(
                mine[:, pl.ds(at_multiple(keep + at, tile), tile)]
            )
            target[:, pl.ds(at_multiple(place + at, tile), tile)] = value.astype(jnp.bfloat16)
            return carry

        if widths[level] == tile:
            add(0, 0)
        else:
            lax.fori_loop(0, widths[level] // tile, add, 0)

    def kept(c, level):
        base = block_of(c)[1]
        return pl.ds(at_multiple(base + offsets[level], widths[level]), widths[level])

    def gather_start(c, level):
        region = total.at[block_of(c)[0], pl.ds(0, height(c)), kept(c, level)]
        send(c, bits + level, region, region, (partner[level], shard))

    def push(block, start):
        def step(i, carry):
            cols = pl.ds(at_multiple(start + i * TILE, TILE), TILE)
            summed_grad = wide(total[block, :, cols])
            moment_wide = momentum_decay * wide(moment[block, :, cols]) + summed_grad
            moment[block, :, cols] = moment_wide.astype(jnp.bfloat16)
            pushed[block, 0:rows, cols] = (
                summed_grad + momentum_decay * moment_wide
            ).astype(jnp.bfloat16)
            return carry

        lax.fori_loop(0, widths[0] // TILE, step, 0)

    stores = []

    def store(src, dst, slot):
        copy = pltpu.make_async_copy(src, dst, local_sem.at[slot])
        copy.start()
        stores.append(copy)

    def group_stage(c, s):
        block, base = block_of(c)
        if s == 0:
            scatter_start(c, 0)
        elif s < bits:
            scatter_finish(c, s - 1)
            scatter_start(c, s)
        elif s == bits:
            scatter_finish(c, bits - 1)
            gather_start(c, bits - 1)
        elif s < 2 * bits:
            level = 2 * bits - s
            started[(c, bits + level)].wait_recv()
            gather_start(c, level - 1)
            if level == 1 and block < MATS:
                ready("moment")
                push(block, base + offsets[0])
                send(
                    c,
                    2 * bits,
                    pushed.at[block, pl.ds(0, rows), kept(c, 0)],
                    pushed.at[block, pl.ds(rows, rows), kept(c, 0)],
                    (me, other_shard),
                )
        else:
            started[(c, bits)].wait_recv()
            if block < MATS:
                push(block, base + widths[0] - offsets[0])
                if c % PIECES == PIECES - 1:
                    store(moment.at[block], new_moment_hbm.at[block], 3 + MATS + block)
            else:
                cols = pl.ds(base, width)
                small_out[:, cols] = total[block, 0:SMALL_ROWS, cols]

    def shard_stage(c, s):
        block, base = block_of(c)
        if s == 0:
            started[(c, 2 * bits)].wait_recv()
            region = pushed.at[block, pl.ds(rows, rows), kept(c, 0)]
            send(c, 2 * bits + 1, region, region, (partner[0], shard))
        else:
            started[(c, 2 * bits + 1)].wait_recv()
            piece = pushed[block, :, base : base + width]
            value = lax.dot_general(
                piece, piece, (((1,), (1,)), ((), ())), preferred_element_type=jnp.float32
            )
            gram0[block] = value if c % PIECES == 0 else gram0[block] + value

    def narrow_dot(left, right):
        return jnp.dot(
            left.astype(jnp.bfloat16),
            right.astype(jnp.bfloat16),
            preferred_element_type=jnp.float32,
        )

    def full_sum(value):
        return jnp.sum(jnp.sum(value, axis=1, keepdims=True), axis=0, keepdims=True)

    muon_scale = 0.2 * math.sqrt(max(HEAD, D))
    batch = MATS // 2

    def solve_stage(half, s):
        members = range(half * batch, (half + 1) * batch)
        if s < NS_ITERS:
            here = lax.broadcasted_iota(jnp.int32, (HEAD, HEAD), 0)
            there = lax.broadcasted_iota(jnp.int32, (HEAD, HEAD), 1)
            eye = jnp.where(here == there, 1.0, 0.0).astype(jnp.float32)
            grams, scales = [], []
            for c in members:
                if s == 0 or s == NS_ITERS - 1:
                    scale = 1.0 / (jnp.sqrt(full_sum(gram0[c] * eye)) + norm_epsilon)
                    scales.append(scale)
                grams.append(gram0[c] * scale * scale if s == 0 else gram[c])
            squares = [narrow_dot(g, g) for g in grams]
            blends = [
                quintic_a * eye + quintic_b * g + quintic_c * q for g, q in zip(grams, squares)
            ]
            if s == 0:
                products = blends
            else:
                products = [narrow_dot(b, product[c]) for b, c in zip(blends, members)]
            if s < NS_ITERS - 1:
                halves = [narrow_dot(b, g) for b, g in zip(blends, grams)]
                grams = [narrow_dot(h, b) for h, b in zip(halves, blends)]
                for c, p, g in zip(members, products, grams):
                    product[c] = p
                    gram[c] = g
            else:
                for c, p, scale in zip(members, products, scales):
                    scaled = p * scale
                    energy = full_sum(scaled * gram0[c]) / (HEAD * math.sqrt(D))
                    energy_out[pl.ds(c, 1), :] = jnp.broadcast_to(energy, (1, 128))
                    polynomial[c] = scaled[0:rows].astype(jnp.bfloat16)
            return
        c = members[s - NS_ITERS]
        ready("weight")

        def update(i, carry):
            cols = pl.ds(at_multiple(i * TILE, TILE), TILE)
            ortho = jnp.dot(
                polynomial[c], pushed[c, :, cols], preferred_element_type=jnp.float32
            ).astype(jnp.bfloat16)
            weight[c, :, cols] = (
                wide(weight[c, :, cols]) * (1.0 - muon_rate * weight_decay)
                - muon_rate * muon_scale * wide(ortho)
            ).astype(jnp.bfloat16)
            return carry

        lax.fori_loop(0, weight.shape[2] // TILE, update, 0)
        store(weight.at[c], new_weight_hbm.at[c], 3 + 2 * MATS + c)

    count = [0] * (2 * chains + 2)
    for code in ORDER:
        s = count[code]
        count[code] += 1
        if code < chains:
            group_stage(code, s)
        elif code < 2 * chains:
            shard_stage(code - chains, s)
        else:
            solve_stage(code - 2 * chains, s)
    for copy in started.values():
        copy.wait_send()
    for copy in stores:
        copy.wait()


def finish_kernel(
    owners,
    small,
    energy,
    weight_hbm,
    moment_hbm,
    *refs,
):
    adam, outs = refs[:9], refs[9:-1]
    sem = refs[-1]
    new_weight, new_moment, owner_sums = outs[:3]
    copies = []
    for b in range(MATS):
        for slot, src, dst in ((0, weight_hbm, new_weight), (1, moment_hbm, new_moment)):
            copy = pltpu.make_async_copy(src.at[b], dst.at[b], sem.at[slot, b])
            copy.start()
            copies.append(copy)
    shard = lax.axis_index("shard")
    lane = lax.broadcasted_iota(jnp.int32, (1, 128), 1)
    row = jnp.zeros((1, 128), jnp.float32)
    for i in range(MATS):
        slot = owners[i] * HALF_MATS
        for j in range(i):
            slot = slot + jnp.where(owners[j] == owners[i], 1, 0)
        row = row + jnp.where(lane == slot - shard * HALF_MATS, energy[i : i + 1, :], 0.0)
    owner_sums[...] = row[:, 0:HALF_MATS]
    emb_rows = adam[0].shape[0]
    gains = adam[3].shape[1]
    heads = adam[6].shape[1]

    def emb_step(i, carry):
        cols = pl.ds(pl.multiple_of(i * TILE, TILE), TILE)
        results = adamw(
            adam[0][:, cols], wide(small[0:emb_rows, cols]), adam[1][:, cols], adam[2][:, cols]
        )
        for ref, result in zip(outs[3:6], results):
            ref[:, cols] = result
        return carry

    lax.fori_loop(0, adam[0].shape[1] // TILE, emb_step, 0)
    extra = wide(small[emb_rows:SMALL_ROWS, 0 : gains + heads])
    for k, cols in ((1, slice(0, gains)), (2, slice(gains, gains + heads))):
        weight, first, second = adam[3 * k : 3 * k + 3]
        results = adamw(weight[...], extra[0:2, cols], first[...], second[...])
        for ref, result in zip(outs[3 + 3 * k : 6 + 3 * k], results):
            ref[...] = result
    for copy in copies:
        copy.wait()


def linked_device(
    groups,
    owners,
    mat_weight,
    mat_grad,
    head_block_momentum,
    emb_weight,
    emb_grad,
    emb_first,
    emb_second,
    norm_weight,
    norm_grad,
    norm_first,
    norm_second,
    qk_weight,
    qk_grad,
    qk_first,
    qk_second,
):
    bits = groups.bit_length() - 1
    blocks, rows, width = mat_weight.shape
    levels = [width // PIECES >> (level + 1) for level in range(bits)]
    chains = (blocks + 1) * PIECES
    in_vmem = pl.BlockSpec(memory_space=pltpu.VMEM)
    anywhere = pl.BlockSpec(memory_space=pl.ANY)
    block_shape = (blocks, rows, width)
    new_weight, new_moment, small_sum, energy = pl.pallas_call(
        functools.partial(linked_kernel, bits),
        out_shape=(
            jax.ShapeDtypeStruct(block_shape, jnp.bfloat16),
            jax.ShapeDtypeStruct(block_shape, jnp.bfloat16),
            jax.ShapeDtypeStruct((SMALL_ROWS, width), jnp.bfloat16),
            jax.ShapeDtypeStruct((8, 128), jnp.float32),
        ),
        in_specs=[in_vmem] * 2 + [anywhere] * 4,
        out_specs=(anywhere, anywhere, in_vmem, in_vmem),
        scratch_shapes=[
            pltpu.VMEM(block_shape, jnp.bfloat16),
            pltpu.VMEM(block_shape, jnp.bfloat16),
            pltpu.VMEM(block_shape, jnp.bfloat16),
            pltpu.VMEM((SMALL_ROWS, width), jnp.bfloat16),
            pltpu.VMEM((blocks + 1, rows, width), jnp.bfloat16),
            pltpu.VMEM((blocks, 2 * rows, width), jnp.bfloat16),
            pltpu.VMEM((blocks, HEAD, HEAD), jnp.float32),
            pltpu.VMEM((blocks, HEAD, HEAD), jnp.float32),
            pltpu.VMEM((blocks, HEAD, HEAD), jnp.float32),
            pltpu.VMEM((blocks, rows, HEAD), jnp.bfloat16),
            pltpu.SemaphoreType.DMA((3 + 3 * blocks,)),
            pltpu.SemaphoreType.DMA((chains, 2 * bits + 2)),
            pltpu.SemaphoreType.DMA((chains, 2 * bits + 2)),
        ]
        + [pltpu.VMEM((chains, rows, part), jnp.bfloat16) for part in levels]
        + [pltpu.VMEM((chains, rows, part), jnp.bfloat16) for part in levels[:-1]],
        compiler_params=pltpu.CompilerParams(
            collective_id=0, has_side_effects=True, vmem_limit_bytes=56 * 1024 * 1024
        ),
    )(norm_grad[0], qk_grad[0], mat_grad[0], emb_grad[0], head_block_momentum, mat_weight)
    adam = (
        emb_weight,
        emb_first,
        emb_second,
        norm_weight,
        norm_first,
        norm_second,
        qk_weight,
        qk_first,
        qk_second,
    )
    return pl.pallas_call(
        finish_kernel,
        out_shape=(
            jax.ShapeDtypeStruct(block_shape, jnp.bfloat16),
            jax.ShapeDtypeStruct(block_shape, jnp.bfloat16),
            jax.ShapeDtypeStruct((1, HALF_MATS), jnp.float32),
        )
        + tuple(jax.ShapeDtypeStruct(a.shape, a.dtype) for a in adam),
        in_specs=[pl.BlockSpec(memory_space=pltpu.SMEM), in_vmem, in_vmem, anywhere, anywhere]
        + [in_vmem] * 9,
        out_specs=(anywhere, anywhere) + (in_vmem,) * 10,
        scratch_shapes=[pltpu.SemaphoreType.DMA((2, blocks))],
        compiler_params=pltpu.CompilerParams(vmem_limit_bytes=32 * 1024 * 1024),
    )(owners, small_sum, energy, new_weight, new_moment, *adam)


def solution(mesh):
    plan = on_device
    if links_fit(mesh.shape["group"], mesh.shape["shard"]):
        plan = functools.partial(linked_device, mesh.shape["group"])
    placed = (
        P(),
        P(None, "shard", None),
        P("group", None, "shard", None),
        P(None, "shard", None),
        P("shard", None),
        P("group", "shard", None),
        P("shard", None),
        P("shard", None),
        P(None, "shard"),
        P("group", None, "shard"),
        P(None, "shard"),
        P(None, "shard"),
        P(),
        P("group", None, None),
        P(),
        P(),
    )
    return jax.shard_map(
        plan,
        mesh=mesh,
        in_specs=placed,
        out_specs=(
            P(None, "shard", None),
            P(None, "shard", None),
            P("shard", None),
            P("shard", None),
            P("shard", None),
            P("shard", None),
            P(None, "shard"),
            P(None, "shard"),
            P(None, "shard"),
            P(),
            P(),
            P(),
        ),
        check_vma=False,
    )
```

```python
import math

import jax
import jax.numpy as jnp
from jax import lax
from jax.experimental import pallas as pl
from jax.experimental.pallas import tpu as pltpu
from jax.sharding import PartitionSpec as P

D = 4096
HEAD = 128
MATS = 6
NS_ITERS = 5


momentum_decay = 0.95
muon_rate = 0.02
weight_decay = 0.1
adam_rate = 0.01
beta_first = 0.9
beta_second = 0.95
adam_epsilon = 1e-08
bias_first = 1.0 - 0.9**10
bias_second = 1.0 - 0.95**10
norm_epsilon = 1e-07
quintic_a = 3.4445
quintic_b = -4.775
quintic_c = 2.0315


def orthogonalize(matrix):
    widened = matrix.astype(jnp.float32)
    iterate = (widened / (jnp.sqrt(jnp.sum(widened * widened)) + norm_epsilon)).astype(jnp.bfloat16)
    for sweep in range(NS_ITERS):
        gram = jnp.dot(iterate, iterate.T, preferred_element_type=jnp.float32).astype(jnp.bfloat16)
        squared = jnp.dot(gram, gram, preferred_element_type=jnp.float32)
        blend = (quintic_b * gram.astype(jnp.float32) + quintic_c * squared).astype(jnp.bfloat16)
        iterate = (
            quintic_a * iterate.astype(jnp.float32)
            + jnp.dot(blend, iterate, preferred_element_type=jnp.float32)
        ).astype(jnp.bfloat16)
    return iterate


def slot_energy(ortho, pushed):
    return jnp.sum(ortho.astype(jnp.float32) * pushed.astype(jnp.float32), axis=(1, 2)) / (
        HEAD * math.sqrt(D)
    )


def owner_slots(owners, capacity):
    order = jnp.arange(owners.shape[0], dtype=jnp.int32)
    same = (owners[:, None] == owners[None, :]) & (order[None, :] < order[:, None])
    position = jnp.sum(same.astype(jnp.int32), axis=1)
    return owners * capacity + position


def adamw(weight, grad_sum, first, second):
    first_new = beta_first * first + (1.0 - beta_first) * grad_sum
    second_new = beta_second * second + (1.0 - beta_second) * grad_sum * grad_sum
    wide_weight = weight.astype(jnp.float32)
    stepped = (
        first_new / bias_first / (jnp.sqrt(second_new / bias_second) + adam_epsilon)
        + weight_decay * wide_weight
    )
    return ((wide_weight - adam_rate * stepped).astype(jnp.bfloat16), first_new, second_new)


def on_device(
    owners,
    mat_weight,
    mat_grad,
    head_block_momentum,
    emb_weight,
    emb_grad,
    emb_first,
    emb_second,
    norm_weight,
    norm_grad,
    norm_first,
    norm_second,
    qk_weight,
    qk_grad,
    qk_first,
    qk_second,
):
    shards = lax.axis_size("shard")
    capacity = -(-MATS // shards)
    rows = mat_weight.shape[1]
    width = mat_weight.shape[2]
    muon_scale = 0.2 * math.sqrt(max(HEAD, D))
    local_grad = mat_grad[0].astype(jnp.float32)
    grad_total, emb_total, norm_total, qk_total = lax.psum(
        (
            local_grad,
            emb_grad[0].astype(jnp.float32),
            norm_grad[0].astype(jnp.float32),
            qk_grad[0].astype(jnp.float32),
        ),
        "group",
    )
    moment_wide = momentum_decay * head_block_momentum.astype(jnp.float32) + grad_total
    new_moment = moment_wide.astype(jnp.bfloat16)
    forwarded_rows = (grad_total + momentum_decay * moment_wide).astype(jnp.bfloat16)
    slots = owner_slots(owners, capacity)
    places = jnp.arange(shards * capacity, dtype=jnp.int32)
    gather_rows_back = (slots[:, None] == places[None, :]).astype(jnp.bfloat16)
    outgoing = jnp.einsum(
        "of,oyq->fyq", gather_rows_back, forwarded_rows, preferred_element_type=jnp.float32
    ).astype(jnp.bfloat16)
    outgoing = outgoing.reshape(shards, capacity, rows, width)
    items = lax.all_to_all(outgoing, "shard", split_axis=0, concat_axis=2, tiled=True)
    ortho = lax.map(orthogonalize, items[0])
    returned = lax.all_to_all(ortho[None], "shard", split_axis=2, concat_axis=0, tiled=True)
    returned, owner_sums = (returned, slot_energy(ortho, items[0])[None])
    kept_row_block = returned.reshape(shards * capacity, rows, width)
    muon_update = jnp.einsum(
        "ar,rpx->apx", gather_rows_back, kept_row_block, preferred_element_type=jnp.float32
    )
    new_weight = (
        mat_weight.astype(jnp.float32) * (1.0 - muon_rate * weight_decay)
        - muon_rate * muon_scale * muon_update
    ).astype(jnp.bfloat16)
    emb_new, emb_first_new, emb_second_new = adamw(emb_weight, emb_total, emb_first, emb_second)
    norm_new, norm_first_new, norm_second_new = adamw(
        norm_weight, norm_total, norm_first, norm_second
    )
    qk_new, qk_first_new, qk_second_new = adamw(qk_weight, qk_total, qk_first, qk_second)
    return (
        new_weight,
        new_moment,
        owner_sums,
        emb_new,
        emb_first_new,
        emb_second_new,
        norm_new,
        norm_first_new,
        norm_second_new,
        qk_new,
        qk_first_new,
        qk_second_new,
    )


SMALL_ROWS = 48
HALF_MATS = -(-MATS // 2)
TILE = 512
PIECES = 2
ORDER = (
    0, 1, 2, 3, 4, 5, 6, 7, 8, 9, 10, 11, 12, 13, 0, 1, 2, 3, 4, 5, 6, 7, 0, 1, 2, 3, 0, 4, 1,
    5, 2, 6, 3, 7, 0, 8, 4, 1, 9, 5, 0, 2, 10, 8, 6, 1, 0, 3, 11, 9, 7, 2, 1, 4, 12, 10, 14,
    5, 13, 3, 2, 8, 11, 15, 14, 4, 3, 6, 9, 12, 16, 5, 7, 15, 4, 10, 13, 17, 8, 16, 6, 5, 7,
    11, 18, 9, 17, 19, 12, 8, 6, 7, 10, 18, 13, 19, 9, 8, 11, 12, 20, 28, 21, 28, 10, 9, 13,
    20, 22, 28, 11, 12, 10, 21, 23, 28, 13, 22, 11, 12, 24, 28, 23, 13, 28, 25, 28, 24, 28,
    25, 29, 29, 29, 29, 29, 29, 29, 29,
)
BATCHES = ((0, 1, 2), (3, 4, 5))
HALVINGS = 2
LINE = 4
GATHER, EXCHANGE, RELAY, SLOTS = 5, 10, 11, 12


def links_fit(groups, shards):
    return groups == LINE << HALVINGS and shards == 2


def wide(value):
    return value.astype(jnp.float32)


def linked_kernel(
    norm_ref,
    qk_ref,
    grad_hbm,
    emb_hbm,
    moment_hbm,
    weight_hbm,
    new_weight_hbm,
    new_moment_hbm,
    small_out,
    energy_out,
    grad,
    moment,
    weight,
    small,
    total,
    pushed,
    gram0,
    gram,
    product,
    polynomial,
    local_sem,
    send_sem,
    recv_sem,
    *levels,
):
    landed, line_landed, summed = levels[:HALVINGS], levels[HALVINGS], levels[HALVINGS + 1 :]
    rows, width = grad.shape[1], grad.shape[2] // PIECES
    chains = (MATS + 1) * PIECES
    widths = [width >> (level + 1) for level in range(HALVINGS)]
    piece = widths[-1] // LINE
    me = lax.axis_index("group")
    shard = lax.axis_index("shard")
    digit = [lax.rem(lax.div(me, 1 << b), 2) for b in range(HALVINGS)]
    partner = [me + (1 << b) * (1 - 2 * digit[b]) for b in range(HALVINGS)]
    spot = lax.div(me, 1 << HALVINGS)
    peer_spot = [lax.rem(spot + step, LINE) for step in range(1, LINE)]
    peers = [me + (there - spot) * (1 << HALVINGS) for there in peer_spot]
    other_shard = 1 - shard
    offsets = []
    for level in range(HALVINGS):
        before = offsets[-1] if offsets else 0
        offsets.append(before + digit[level] * widths[level])

    barrier = pltpu.get_barrier_semaphore()
    for device in partner + peers:
        pl.semaphore_signal(
            barrier, inc=1, device_id=(device, shard), device_id_type=pl.DeviceIdType.MESH
        )
    pl.semaphore_signal(
        barrier, inc=1, device_id=(me, other_shard), device_id_type=pl.DeviceIdType.MESH
    )
    loads = {("grad", b): pltpu.make_async_copy(
        grad_hbm.at[b], grad.at[b], local_sem.at[3 + b]) for b in range(MATS)}
    loads["small"] = pltpu.make_async_copy(
        emb_hbm, small.at[pl.ds(0, emb_hbm.shape[0])], local_sem.at[0])
    loads["moment"] = pltpu.make_async_copy(moment_hbm, moment, local_sem.at[1])
    loads["weight"] = pltpu.make_async_copy(weight_hbm, weight, local_sem.at[2])
    for load in loads.values():
        load.start()
    extra = SMALL_ROWS - emb_hbm.shape[0]
    small[pl.ds(emb_hbm.shape[0], extra), :] = jnp.zeros((extra, small.shape[1]), jnp.bfloat16)
    place = 0
    for part in (norm_ref, qk_ref):
        tall = jnp.concatenate(
            [wide(part[...]), jnp.zeros((extra - 2, part.shape[1]), jnp.float32)], axis=0
        )
        small[pl.ds(emb_hbm.shape[0], extra), pl.ds(place, part.shape[1])] = tall.astype(
            jnp.bfloat16
        )
        place += part.shape[1]
    pl.semaphore_wait(barrier, len(partner) + len(peers) + 1)

    def ready(key):
        if key in loads:
            loads.pop(key).wait()

    started = {}

    def send(c, slot, src, dst, device):
        copy = pltpu.make_async_remote_copy(
            src_ref=src,
            dst_ref=dst,
            send_sem=send_sem.at[c, slot],
            recv_sem=recv_sem.at[c, slot],
            device_id=device,
            device_id_type=pl.DeviceIdType.MESH,
        )
        copy.start()
        started[(c, slot)] = copy

    def block_of(c):
        return c // PIECES, (c % PIECES) * width

    def height(c):
        return rows if c < MATS * PIECES else SMALL_ROWS

    def held(c, level, own):
        block, base = block_of(c)
        if level >= 0:
            return summed[level].at[c, pl.ds(0, height(c))], 0
        if block == MATS:
            return small, base
        return (grad if own else grad_hbm).at[block], base

    def at_multiple(value, step):
        return value if isinstance(value, int) else pl.multiple_of(value, step)

    def scatter_start(c, level):
        if block_of(c)[0] == MATS:
            ready("small")
        source, base = held(c, level - 1, False)
        start = at_multiple(base + (1 - digit[level]) * widths[level], widths[level])
        send(
            c,
            level,
            source.at[:, pl.ds(start, widths[level])],
            landed[level].at[c, pl.ds(0, height(c))],
            (partner[level], shard),
        )

    def scatter_finish(c, level):
        block, base = block_of(c)
        if level == 0:
            ready(("grad", block))
        started[(c, level)].wait_recv()
        mine, keep = held(c, level - 1, True)
        keep = keep + digit[level] * widths[level]
        tile = min(TILE, widths[level])
        arrived = landed[level].at[c, pl.ds(0, height(c))]
        target = summed[level].at[c, pl.ds(0, height(c))]

        def add(i, carry):
            at = at_multiple(i * tile, tile)
            value = wide(arrived[:, pl.ds(at, tile)]) + wide(
                mine[:, pl.ds(at_multiple(keep + at, tile), tile)]
            )
            target[:, pl.ds(at, tile)] = value.astype(jnp.bfloat16)
            return carry

        if widths[level] == tile:
            add(0, 0)
        else:
            lax.fori_loop(0, widths[level] // tile, add, 0)

    def kept(c, level):
        base = block_of(c)[1]
        return pl.ds(at_multiple(base + offsets[level], widths[level]), widths[level])

    def line_scatter(c):
        for k in range(LINE - 1):
            start = at_multiple(peer_spot[k] * piece, piece)
            send(
                c,
                HALVINGS + k,
                summed[-1].at[c, pl.ds(0, height(c)), pl.ds(start, piece)],
                line_landed.at[c, k, pl.ds(0, height(c))],
                (peers[k], shard),
            )

    def line_gather(c):
        block, base = block_of(c)
        value = wide(
            summed[-1][c, 0 : height(c), pl.ds(at_multiple(spot * piece, piece), piece)]
        )
        for k in range(LINE - 1):
            started[(c, HALVINGS + k)].wait_recv()
            value = value + wide(line_landed[c, k, 0 : height(c)])
        start = at_multiple(base + offsets[-1] + spot * piece, piece)
        region = total.at[block, pl.ds(0, height(c)), pl.ds(start, piece)]
        region[...] = value.astype(jnp.bfloat16)
        for k in range(LINE - 1):
            send(c, GATHER + k, region, region, (peers[k], shard))

    def gather_start(c, level):
        region = total.at[block_of(c)[0], pl.ds(0, height(c)), kept(c, level)]
        send(c, EXCHANGE - 1 - level, region, region, (partner[level], shard))

    def push(block, start):
        def step(i, carry):
            cols = pl.ds(at_multiple(start + i * TILE, TILE), TILE)
            summed_grad = wide(total[block, :, cols])
            moment_wide = momentum_decay * wide(moment[block, :, cols]) + summed_grad
            moment[block, :, cols] = moment_wide.astype(jnp.bfloat16)
            pushed[block, 0:rows, cols] = (
                summed_grad + momentum_decay * moment_wide
            ).astype(jnp.bfloat16)
            return carry

        lax.fori_loop(0, widths[0] // TILE, step, 0)

    stores = []

    def store(src, dst, slot):
        copy = pltpu.make_async_copy(src, dst, local_sem.at[slot])
        copy.start()
        stores.append(copy)

    def group_stage(c, s):
        block, base = block_of(c)
        if s == 0:
            scatter_start(c, 0)
        elif s == 1:
            scatter_finish(c, 0)
            scatter_start(c, 1)
        elif s == 2:
            scatter_finish(c, 1)
            line_scatter(c)
        elif s == 3:
            line_gather(c)
        elif s == 4:
            for k in range(LINE - 1):
                started[(c, GATHER + k)].wait_recv()
            gather_start(c, 1)
        elif s == 5:
            started[(c, EXCHANGE - 2)].wait_recv()
            gather_start(c, 0)
            if block < MATS:
                ready("moment")
                push(block, base + offsets[0])
                send(
                    c,
                    EXCHANGE,
                    pushed.at[block, pl.ds(0, rows), kept(c, 0)],
                    pushed.at[block, pl.ds(rows, rows), kept(c, 0)],
                    (me, other_shard),
                )
        else:
            started[(c, EXCHANGE - 1)].wait_recv()
            if block < MATS:
                push(block, base + widths[0] - offsets[0])
                if c % PIECES == PIECES - 1:
                    store(moment.at[block], new_moment_hbm.at[block], 3 + MATS + block)
            else:
                cols = pl.ds(base, width)
                small_out[:, cols] = total[block, 0:SMALL_ROWS, cols]

    def shard_stage(c, s):
        block, base = block_of(c)
        if s == 0:
            started[(c, EXCHANGE)].wait_recv()
            region = pushed.at[block, pl.ds(rows, rows), kept(c, 0)]
            send(c, RELAY, region, region, (partner[0], shard))
        else:
            started[(c, RELAY)].wait_recv()
            part = pushed[block, :, base : base + width]
            value = lax.dot_general(
                part, part, (((1,), (1,)), ((), ())), preferred_element_type=jnp.float32
            )
            gram0[block] = value if c % PIECES == 0 else gram0[block] + value

    def narrow_dot(left, right):
        return jnp.dot(
            left.astype(jnp.bfloat16),
            right.astype(jnp.bfloat16),
            preferred_element_type=jnp.float32,
        )

    def full_sum(value):
        return jnp.sum(jnp.sum(value, axis=1, keepdims=True), axis=0, keepdims=True)

    muon_scale = 0.2 * math.sqrt(max(HEAD, D))

    def solve_stage(batch, s):
        members = BATCHES[batch]
        if s < NS_ITERS:
            here = lax.broadcasted_iota(jnp.int32, (HEAD, HEAD), 0)
            there = lax.broadcasted_iota(jnp.int32, (HEAD, HEAD), 1)
            eye = jnp.where(here == there, 1.0, 0.0).astype(jnp.float32)
            grams, scales = [], []
            for c in members:
                if s == 0 or s == NS_ITERS - 1:
                    scale = 1.0 / (jnp.sqrt(full_sum(gram0[c] * eye)) + norm_epsilon)
                    scales.append(scale)
                grams.append(gram0[c] * scale * scale if s == 0 else gram[c])
            squares = [narrow_dot(g, g) for g in grams]
            blends = [
                quintic_a * eye + quintic_b * g + quintic_c * q for g, q in zip(grams, squares)
            ]
            if s == 0:
                products = blends
            else:
                products = [narrow_dot(b, product[c]) for b, c in zip(blends, members)]
            if s < NS_ITERS - 1:
                halves = [narrow_dot(b, g) for b, g in zip(blends, grams)]
                grams = [narrow_dot(h, b) for h, b in zip(halves, blends)]
                for c, p, g in zip(members, products, grams):
                    product[c] = p
                    gram[c] = g
            else:
                for c, p, scale in zip(members, products, scales):
                    scaled = p * scale
                    energy = full_sum(scaled * gram0[c]) / (HEAD * math.sqrt(D))
                    energy_out[pl.ds(c, 1), :] = jnp.broadcast_to(energy, (1, 128))
                    polynomial[c] = scaled[0:rows].astype(jnp.bfloat16)
            return
        c = members[s - NS_ITERS]
        ready("weight")

        def update(i, carry):
            cols = pl.ds(at_multiple(i * TILE, TILE), TILE)
            ortho = jnp.dot(
                polynomial[c], pushed[c, :, cols], preferred_element_type=jnp.float32
            ).astype(jnp.bfloat16)
            weight[c, :, cols] = (
                wide(weight[c, :, cols]) * (1.0 - muon_rate * weight_decay)
                - muon_rate * muon_scale * wide(ortho)
            ).astype(jnp.bfloat16)
            return carry

        lax.fori_loop(0, weight.shape[2] // TILE, update, 0)
        store(weight.at[c], new_weight_hbm.at[c], 3 + 2 * MATS + c)

    count = [0] * (2 * chains + len(BATCHES))
    for code in ORDER:
        s = count[code]
        count[code] += 1
        if code < chains:
            group_stage(code, s)
        elif code < 2 * chains:
            shard_stage(code - chains, s)
        else:
            solve_stage(code - 2 * chains, s)
    for copy in started.values():
        copy.wait_send()
    for copy in stores:
        copy.wait()


def finish_kernel(
    owners,
    small,
    energy,
    weight_hbm,
    moment_hbm,
    *refs,
):
    adam, outs = refs[:9], refs[9:-1]
    sem = refs[-1]
    new_weight, new_moment, owner_sums = outs[:3]
    copies = []
    for b in range(MATS):
        for slot, src, dst in ((0, weight_hbm, new_weight), (1, moment_hbm, new_moment)):
            copy = pltpu.make_async_copy(src.at[b], dst.at[b], sem.at[slot, b])
            copy.start()
            copies.append(copy)
    shard = lax.axis_index("shard")
    lane = lax.broadcasted_iota(jnp.int32, (1, 128), 1)
    row = jnp.zeros((1, 128), jnp.float32)
    for i in range(MATS):
        slot = owners[i] * HALF_MATS
        for j in range(i):
            slot = slot + jnp.where(owners[j] == owners[i], 1, 0)
        row = row + jnp.where(lane == slot - shard * HALF_MATS, energy[i : i + 1, :], 0.0)
    owner_sums[...] = row[:, 0:HALF_MATS]
    emb_rows = adam[0].shape[0]
    gains = adam[3].shape[1]
    heads = adam[6].shape[1]

    def emb_step(i, carry):
        cols = pl.ds(pl.multiple_of(i * TILE, TILE), TILE)
        results = adamw(
            adam[0][:, cols], wide(small[0:emb_rows, cols]), adam[1][:, cols], adam[2][:, cols]
        )
        for ref, result in zip(outs[3:6], results):
            ref[:, cols] = result
        return carry

    lax.fori_loop(0, adam[0].shape[1] // TILE, emb_step, 0)
    extra = wide(small[emb_rows:SMALL_ROWS, 0 : gains + heads])
    for k, cols in ((1, slice(0, gains)), (2, slice(gains, gains + heads))):
        weight, first, second = adam[3 * k : 3 * k + 3]
        results = adamw(weight[...], extra[0:2, cols], first[...], second[...])
        for ref, result in zip(outs[3 + 3 * k : 6 + 3 * k], results):
            ref[...] = result
    for copy in copies:
        copy.wait()


def linked_device(
    owners,
    mat_weight,
    mat_grad,
    head_block_momentum,
    emb_weight,
    emb_grad,
    emb_first,
    emb_second,
    norm_weight,
    norm_grad,
    norm_first,
    norm_second,
    qk_weight,
    qk_grad,
    qk_first,
    qk_second,
):
    blocks, rows, width = mat_weight.shape
    levels = [width // PIECES >> (level + 1) for level in range(HALVINGS)]
    chains = (blocks + 1) * PIECES
    in_vmem = pl.BlockSpec(memory_space=pltpu.VMEM)
    anywhere = pl.BlockSpec(memory_space=pl.ANY)
    block_shape = (blocks, rows, width)
    new_weight, new_moment, small_sum, energy = pl.pallas_call(
        linked_kernel,
        out_shape=(
            jax.ShapeDtypeStruct(block_shape, jnp.bfloat16),
            jax.ShapeDtypeStruct(block_shape, jnp.bfloat16),
            jax.ShapeDtypeStruct((SMALL_ROWS, width), jnp.bfloat16),
            jax.ShapeDtypeStruct((8, 128), jnp.float32),
        ),
        in_specs=[in_vmem] * 2 + [anywhere] * 4,
        out_specs=(anywhere, anywhere, in_vmem, in_vmem),
        scratch_shapes=[
            pltpu.VMEM(block_shape, jnp.bfloat16),
            pltpu.VMEM(block_shape, jnp.bfloat16),
            pltpu.VMEM(block_shape, jnp.bfloat16),
            pltpu.VMEM((SMALL_ROWS, width), jnp.bfloat16),
            pltpu.VMEM((blocks + 1, rows, width), jnp.bfloat16),
            pltpu.VMEM((blocks, 2 * rows, width), jnp.bfloat16),
            pltpu.VMEM((blocks, HEAD, HEAD), jnp.float32),
            pltpu.VMEM((blocks, HEAD, HEAD), jnp.float32),
            pltpu.VMEM((blocks, HEAD, HEAD), jnp.float32),
            pltpu.VMEM((blocks, rows, HEAD), jnp.bfloat16),
            pltpu.SemaphoreType.DMA((3 + 3 * blocks,)),
            pltpu.SemaphoreType.DMA((chains, SLOTS)),
            pltpu.SemaphoreType.DMA((chains, SLOTS)),
        ]
        + [pltpu.VMEM((chains, rows, part), jnp.bfloat16) for part in levels]
        + [pltpu.VMEM((chains, LINE - 1, rows, levels[-1] // LINE), jnp.bfloat16)]
        + [pltpu.VMEM((chains, rows, part), jnp.bfloat16) for part in levels],
        compiler_params=pltpu.CompilerParams(
            collective_id=0, has_side_effects=True, vmem_limit_bytes=56 * 1024 * 1024
        ),
    )(norm_grad[0], qk_grad[0], mat_grad[0], emb_grad[0], head_block_momentum, mat_weight)
    adam = (
        emb_weight,
        emb_first,
        emb_second,
        norm_weight,
        norm_first,
        norm_second,
        qk_weight,
        qk_first,
        qk_second,
    )
    return pl.pallas_call(
        finish_kernel,
        out_shape=(
            jax.ShapeDtypeStruct(block_shape, jnp.bfloat16),
            jax.ShapeDtypeStruct(block_shape, jnp.bfloat16),
            jax.ShapeDtypeStruct((1, HALF_MATS), jnp.float32),
        )
        + tuple(jax.ShapeDtypeStruct(a.shape, a.dtype) for a in adam),
        in_specs=[pl.BlockSpec(memory_space=pltpu.SMEM), in_vmem, in_vmem]
        + [anywhere] * 2
        + [in_vmem] * 9,
        out_specs=(anywhere, anywhere) + (in_vmem,) * 10,
        scratch_shapes=[pltpu.SemaphoreType.DMA((2, blocks))],
        compiler_params=pltpu.CompilerParams(vmem_limit_bytes=61 * 1024 * 1024),
    )(owners, small_sum, energy, new_weight, new_moment, *adam)


def solution(mesh):
    plan = on_device
    if links_fit(mesh.shape["group"], mesh.shape["shard"]):
        plan = linked_device
    placed = (
        P(),
        P(None, "shard", None),
        P("group", None, "shard", None),
        P(None, "shard", None),
        P("shard", None),
        P("group", "shard", None),
        P("shard", None),
        P("shard", None),
        P(None, "shard"),
        P("group", None, "shard"),
        P(None, "shard"),
        P(None, "shard"),
        P(),
        P("group", None, None),
        P(),
        P(),
    )
    return jax.shard_map(
        plan,
        mesh=mesh,
        in_specs=placed,
        out_specs=(
            P(None, "shard", None),
            P(None, "shard", None),
            P("shard", None),
            P("shard", None),
            P("shard", None),
            P("shard", None),
            P(None, "shard"),
            P(None, "shard"),
            P(None, "shard"),
            P(),
            P(),
            P(),
        ),
        check_vma=False,
    )
```

```python
import math

import jax
import jax.numpy as jnp
from jax import lax
from jax.experimental import pallas as pl
from jax.experimental.pallas import tpu as pltpu
from jax.sharding import PartitionSpec as P

D = 4096
HEAD = 128
MATS = 6
NS_ITERS = 5


momentum_decay = 0.95
muon_rate = 0.02
weight_decay = 0.1
adam_rate = 0.01
beta_first = 0.9
beta_second = 0.95
adam_epsilon = 1e-08
bias_first = 1.0 - 0.9**10
bias_second = 1.0 - 0.95**10
norm_epsilon = 1e-07
quintic_a = 3.4445
quintic_b = -4.775
quintic_c = 2.0315


def orthogonalize(matrix):
    widened = matrix.astype(jnp.float32)
    iterate = (widened / (jnp.sqrt(jnp.sum(widened * widened)) + norm_epsilon)).astype(jnp.bfloat16)
    for sweep in range(NS_ITERS):
        gram = jnp.dot(iterate, iterate.T, preferred_element_type=jnp.float32).astype(jnp.bfloat16)
        squared = jnp.dot(gram, gram, preferred_element_type=jnp.float32)
        blend = (quintic_b * gram.astype(jnp.float32) + quintic_c * squared).astype(jnp.bfloat16)
        iterate = (
            quintic_a * iterate.astype(jnp.float32)
            + jnp.dot(blend, iterate, preferred_element_type=jnp.float32)
        ).astype(jnp.bfloat16)
    return iterate


def slot_energy(ortho, pushed):
    return jnp.sum(ortho.astype(jnp.float32) * pushed.astype(jnp.float32), axis=(1, 2)) / (
        HEAD * math.sqrt(D)
    )


def owner_slots(owners, capacity):
    order = jnp.arange(owners.shape[0], dtype=jnp.int32)
    same = (owners[:, None] == owners[None, :]) & (order[None, :] < order[:, None])
    position = jnp.sum(same.astype(jnp.int32), axis=1)
    return owners * capacity + position


def adamw(weight, grad_sum, first, second):
    first_new = beta_first * first + (1.0 - beta_first) * grad_sum
    second_new = beta_second * second + (1.0 - beta_second) * grad_sum * grad_sum
    wide_weight = weight.astype(jnp.float32)
    stepped = (
        first_new / bias_first / (jnp.sqrt(second_new / bias_second) + adam_epsilon)
        + weight_decay * wide_weight
    )
    return ((wide_weight - adam_rate * stepped).astype(jnp.bfloat16), first_new, second_new)


def on_device(
    owners,
    mat_weight,
    mat_grad,
    head_block_momentum,
    emb_weight,
    emb_grad,
    emb_first,
    emb_second,
    norm_weight,
    norm_grad,
    norm_first,
    norm_second,
    qk_weight,
    qk_grad,
    qk_first,
    qk_second,
):
    shards = lax.axis_size("shard")
    capacity = -(-MATS // shards)
    rows = mat_weight.shape[1]
    width = mat_weight.shape[2]
    muon_scale = 0.2 * math.sqrt(max(HEAD, D))
    local_grad = mat_grad[0].astype(jnp.float32)
    grad_total, emb_total, norm_total, qk_total = lax.psum(
        (
            local_grad,
            emb_grad[0].astype(jnp.float32),
            norm_grad[0].astype(jnp.float32),
            qk_grad[0].astype(jnp.float32),
        ),
        "group",
    )
    moment_wide = momentum_decay * head_block_momentum.astype(jnp.float32) + grad_total
    new_moment = moment_wide.astype(jnp.bfloat16)
    forwarded_rows = (grad_total + momentum_decay * moment_wide).astype(jnp.bfloat16)
    slots = owner_slots(owners, capacity)
    places = jnp.arange(shards * capacity, dtype=jnp.int32)
    gather_rows_back = (slots[:, None] == places[None, :]).astype(jnp.bfloat16)
    outgoing = jnp.einsum(
        "of,oyq->fyq", gather_rows_back, forwarded_rows, preferred_element_type=jnp.float32
    ).astype(jnp.bfloat16)
    outgoing = outgoing.reshape(shards, capacity, rows, width)
    items = lax.all_to_all(outgoing, "shard", split_axis=0, concat_axis=2, tiled=True)
    ortho = lax.map(orthogonalize, items[0])
    returned = lax.all_to_all(ortho[None], "shard", split_axis=2, concat_axis=0, tiled=True)
    returned, owner_sums = (returned, slot_energy(ortho, items[0])[None])
    kept_row_block = returned.reshape(shards * capacity, rows, width)
    muon_update = jnp.einsum(
        "ar,rpx->apx", gather_rows_back, kept_row_block, preferred_element_type=jnp.float32
    )
    new_weight = (
        mat_weight.astype(jnp.float32) * (1.0 - muon_rate * weight_decay)
        - muon_rate * muon_scale * muon_update
    ).astype(jnp.bfloat16)
    emb_new, emb_first_new, emb_second_new = adamw(emb_weight, emb_total, emb_first, emb_second)
    norm_new, norm_first_new, norm_second_new = adamw(
        norm_weight, norm_total, norm_first, norm_second
    )
    qk_new, qk_first_new, qk_second_new = adamw(qk_weight, qk_total, qk_first, qk_second)
    return (
        new_weight,
        new_moment,
        owner_sums,
        emb_new,
        emb_first_new,
        emb_second_new,
        norm_new,
        norm_first_new,
        norm_second_new,
        qk_new,
        qk_first_new,
        qk_second_new,
    )


SMALL_ROWS = 48
HALF_MATS = -(-MATS // 2)
TILE = 512
PIECES = 2
ORDER = (
    0, 1, 2, 3, 4, 5, 6, 7, 8, 9, 10, 11, 12, 13, 0, 1, 2, 3, 4, 5, 6, 7, 0, 1, 2, 0, 3, 1, 4,
    2, 5, 0, 8, 6, 3, 7, 1, 9, 0, 4, 2, 8, 10, 5, 0, 1, 6, 9, 3, 11, 14, 2, 1, 7, 10, 4, 12,
    14, 15, 2, 3, 8, 5, 11, 13, 15, 16, 3, 4, 6, 9, 12, 7, 5, 16, 17, 4, 10, 13, 8, 6, 5, 17,
    18, 7, 11, 9, 6, 12, 8, 19, 18, 7, 10, 13, 9, 8, 19, 20, 11, 28, 12, 28, 9, 10, 21, 20,
    13, 28, 11, 28, 10, 21, 22, 12, 28, 11, 13, 28, 23, 28, 22, 12, 13, 28, 23, 24, 29, 29,
    29, 29, 25, 29, 24, 29, 29, 25, 30, 30, 30, 30, 30, 30,
)
BATCHES = ((0, 1, 2), (3, 4), (5,))
HALVINGS = 2
LINE = 4
GATHER, EXCHANGE, RELAY, SLOTS = 5, 10, 11, 12


def links_fit(groups, shards):
    return groups == LINE << HALVINGS and shards == 2


def wide(value):
    return value.astype(jnp.float32)


def linked_kernel(
    norm_ref,
    qk_ref,
    grad_hbm,
    emb_hbm,
    moment_hbm,
    weight_hbm,
    new_weight_hbm,
    new_moment_hbm,
    small_out,
    energy_out,
    grad,
    moment,
    weight,
    small,
    total,
    pushed,
    gram0,
    gram,
    product,
    polynomial,
    local_sem,
    send_sem,
    recv_sem,
    *levels,
):
    landed, line_landed, summed = levels[:HALVINGS], levels[HALVINGS], levels[HALVINGS + 1 :]
    rows, width = grad.shape[1], grad.shape[2] // PIECES
    chains = (MATS + 1) * PIECES
    widths = [width >> (level + 1) for level in range(HALVINGS)]
    piece = widths[-1] // LINE
    me = lax.axis_index("group")
    shard = lax.axis_index("shard")
    digit = [lax.rem(lax.div(me, 1 << b), 2) for b in range(HALVINGS)]
    partner = [me + (1 << b) * (1 - 2 * digit[b]) for b in range(HALVINGS)]
    spot = lax.div(me, 1 << HALVINGS)
    peer_spot = [lax.rem(spot + step, LINE) for step in range(1, LINE)]
    peers = [me + (there - spot) * (1 << HALVINGS) for there in peer_spot]
    other_shard = 1 - shard
    offsets = []
    for level in range(HALVINGS):
        before = offsets[-1] if offsets else 0
        offsets.append(before + digit[level] * widths[level])

    barrier = pltpu.get_barrier_semaphore()
    for device in partner + peers:
        pl.semaphore_signal(
            barrier, inc=1, device_id=(device, shard), device_id_type=pl.DeviceIdType.MESH
        )
    pl.semaphore_signal(
        barrier, inc=1, device_id=(me, other_shard), device_id_type=pl.DeviceIdType.MESH
    )
    loads = {("grad", b): pltpu.make_async_copy(
        grad_hbm.at[b], grad.at[b], local_sem.at[3 + b]) for b in range(MATS)}
    loads["small"] = pltpu.make_async_copy(
        emb_hbm, small.at[pl.ds(0, emb_hbm.shape[0])], local_sem.at[0])
    loads["moment"] = pltpu.make_async_copy(moment_hbm, moment, local_sem.at[1])
    loads["weight"] = pltpu.make_async_copy(weight_hbm, weight, local_sem.at[2])
    for load in loads.values():
        load.start()
    extra = SMALL_ROWS - emb_hbm.shape[0]
    small[pl.ds(emb_hbm.shape[0], extra), :] = jnp.zeros((extra, small.shape[1]), jnp.bfloat16)
    place = 0
    for part in (norm_ref, qk_ref):
        tall = jnp.concatenate(
            [wide(part[...]), jnp.zeros((extra - 2, part.shape[1]), jnp.float32)], axis=0
        )
        small[pl.ds(emb_hbm.shape[0], extra), pl.ds(place, part.shape[1])] = tall.astype(
            jnp.bfloat16
        )
        place += part.shape[1]
    pl.semaphore_wait(barrier, len(partner) + len(peers) + 1)

    def ready(key):
        if key in loads:
            loads.pop(key).wait()

    started = {}

    def send(c, slot, src, dst, device):
        copy = pltpu.make_async_remote_copy(
            src_ref=src,
            dst_ref=dst,
            send_sem=send_sem.at[c, slot],
            recv_sem=recv_sem.at[c, slot],
            device_id=device,
            device_id_type=pl.DeviceIdType.MESH,
        )
        copy.start()
        started[(c, slot)] = copy

    def block_of(c):
        return c // PIECES, (c % PIECES) * width

    def height(c):
        return rows if c < MATS * PIECES else SMALL_ROWS

    def held(c, level, own):
        block, base = block_of(c)
        if level >= 0:
            return summed[level].at[c, pl.ds(0, height(c))], 0
        if block == MATS:
            return small, base
        return (grad if own else grad_hbm).at[block], base

    def at_multiple(value, step):
        return value if isinstance(value, int) else pl.multiple_of(value, step)

    def scatter_start(c, level):
        if block_of(c)[0] == MATS:
            ready("small")
        source, base = held(c, level - 1, False)
        start = at_multiple(base + (1 - digit[level]) * widths[level], widths[level])
        send(
            c,
            level,
            source.at[:, pl.ds(start, widths[level])],
            landed[level].at[c, pl.ds(0, height(c))],
            (partner[level], shard),
        )

    def scatter_finish(c, level):
        block, base = block_of(c)
        if level == 0:
            ready(("grad", block))
        started[(c, level)].wait_recv()
        mine, keep = held(c, level - 1, True)
        keep = keep + digit[level] * widths[level]
        tile = min(TILE, widths[level])
        arrived = landed[level].at[c, pl.ds(0, height(c))]
        target = summed[level].at[c, pl.ds(0, height(c))]

        def add(i, carry):
            at = at_multiple(i * tile, tile)
            value = wide(arrived[:, pl.ds(at, tile)]) + wide(
                mine[:, pl.ds(at_multiple(keep + at, tile), tile)]
            )
            target[:, pl.ds(at, tile)] = value.astype(jnp.bfloat16)
            return carry

        if widths[level] == tile:
            add(0, 0)
        else:
            lax.fori_loop(0, widths[level] // tile, add, 0)

    def kept(c, level):
        base = block_of(c)[1]
        return pl.ds(at_multiple(base + offsets[level], widths[level]), widths[level])

    def line_scatter(c):
        for k in range(LINE - 1):
            start = at_multiple(peer_spot[k] * piece, piece)
            send(
                c,
                HALVINGS + k,
                summed[-1].at[c, pl.ds(0, height(c)), pl.ds(start, piece)],
                line_landed.at[c, k, pl.ds(0, height(c))],
                (peers[k], shard),
            )

    def line_gather(c):
        block, base = block_of(c)
        value = wide(
            summed[-1][c, 0 : height(c), pl.ds(at_multiple(spot * piece, piece), piece)]
        )
        for k in range(LINE - 1):
            started[(c, HALVINGS + k)].wait_recv()
            value = value + wide(line_landed[c, k, 0 : height(c)])
        start = at_multiple(base + offsets[-1] + spot * piece, piece)
        region = total.at[block, pl.ds(0, height(c)), pl.ds(start, piece)]
        region[...] = value.astype(jnp.bfloat16)
        for k in range(LINE - 1):
            send(c, GATHER + k, region, region, (peers[k], shard))

    def gather_start(c, level):
        region = total.at[block_of(c)[0], pl.ds(0, height(c)), kept(c, level)]
        send(c, EXCHANGE - 1 - level, region, region, (partner[level], shard))

    def push(block, start):
        def step(i, carry):
            cols = pl.ds(at_multiple(start + i * TILE, TILE), TILE)
            summed_grad = wide(total[block, :, cols])
            moment_wide = momentum_decay * wide(moment[block, :, cols]) + summed_grad
            moment[block, :, cols] = moment_wide.astype(jnp.bfloat16)
            pushed[block, 0:rows, cols] = (
                summed_grad + momentum_decay * moment_wide
            ).astype(jnp.bfloat16)
            return carry

        lax.fori_loop(0, widths[0] // TILE, step, 0)

    stores = []

    def store(src, dst, slot):
        copy = pltpu.make_async_copy(src, dst, local_sem.at[slot])
        copy.start()
        stores.append(copy)

    def group_stage(c, s):
        block, base = block_of(c)
        if s == 0:
            scatter_start(c, 0)
        elif s == 1:
            scatter_finish(c, 0)
            scatter_start(c, 1)
        elif s == 2:
            scatter_finish(c, 1)
            line_scatter(c)
        elif s == 3:
            line_gather(c)
        elif s == 4:
            for k in range(LINE - 1):
                started[(c, GATHER + k)].wait_recv()
            gather_start(c, 1)
        elif s == 5:
            started[(c, EXCHANGE - 2)].wait_recv()
            gather_start(c, 0)
            if block < MATS:
                ready("moment")
                push(block, base + offsets[0])
                send(
                    c,
                    EXCHANGE,
                    pushed.at[block, pl.ds(0, rows), kept(c, 0)],
                    pushed.at[block, pl.ds(rows, rows), kept(c, 0)],
                    (me, other_shard),
                )
        else:
            started[(c, EXCHANGE - 1)].wait_recv()
            if block < MATS:
                push(block, base + widths[0] - offsets[0])
                if c % PIECES == PIECES - 1:
                    store(moment.at[block], new_moment_hbm.at[block], 3 + MATS + block)
            else:
                cols = pl.ds(base, width)
                small_out[:, cols] = total[block, 0:SMALL_ROWS, cols]

    def shard_stage(c, s):
        block, base = block_of(c)
        if s == 0:
            started[(c, EXCHANGE)].wait_recv()
            region = pushed.at[block, pl.ds(rows, rows), kept(c, 0)]
            send(c, RELAY, region, region, (partner[0], shard))
        else:
            started[(c, RELAY)].wait_recv()
            part = pushed[block, :, base : base + width]
            value = lax.dot_general(
                part, part, (((1,), (1,)), ((), ())), preferred_element_type=jnp.float32
            )
            gram0[block] = value if c % PIECES == 0 else gram0[block] + value

    def narrow_dot(left, right):
        return jnp.dot(
            left.astype(jnp.bfloat16),
            right.astype(jnp.bfloat16),
            preferred_element_type=jnp.float32,
        )

    def full_sum(value):
        return jnp.sum(jnp.sum(value, axis=1, keepdims=True), axis=0, keepdims=True)

    muon_scale = 0.2 * math.sqrt(max(HEAD, D))

    def solve_stage(batch, s):
        members = BATCHES[batch]
        if s < NS_ITERS:
            here = lax.broadcasted_iota(jnp.int32, (HEAD, HEAD), 0)
            there = lax.broadcasted_iota(jnp.int32, (HEAD, HEAD), 1)
            eye = jnp.where(here == there, 1.0, 0.0).astype(jnp.float32)
            grams, scales = [], []
            for c in members:
                if s == 0 or s == NS_ITERS - 1:
                    scale = 1.0 / (jnp.sqrt(full_sum(gram0[c] * eye)) + norm_epsilon)
                    scales.append(scale)
                grams.append(gram0[c] * scale * scale if s == 0 else gram[c])
            squares = [narrow_dot(g, g) for g in grams]
            blends = [
                quintic_a * eye + quintic_b * g + quintic_c * q for g, q in zip(grams, squares)
            ]
            if s == 0:
                products = blends
            else:
                products = [narrow_dot(b, product[c]) for b, c in zip(blends, members)]
            if s < NS_ITERS - 1:
                halves = [narrow_dot(b, g) for b, g in zip(blends, grams)]
                grams = [narrow_dot(h, b) for h, b in zip(halves, blends)]
                for c, p, g in zip(members, products, grams):
                    product[c] = p
                    gram[c] = g
            else:
                for c, p, scale in zip(members, products, scales):
                    scaled = p * scale
                    energy = full_sum(scaled * gram0[c]) / (HEAD * math.sqrt(D))
                    energy_out[pl.ds(c, 1), :] = jnp.broadcast_to(energy, (1, 128))
                    polynomial[c] = scaled[0:rows].astype(jnp.bfloat16)
            return
        c = members[s - NS_ITERS]
        ready("weight")

        def update(i, carry):
            cols = pl.ds(at_multiple(i * TILE, TILE), TILE)
            ortho = jnp.dot(
                polynomial[c], pushed[c, :, cols], preferred_element_type=jnp.float32
            ).astype(jnp.bfloat16)
            weight[c, :, cols] = (
                wide(weight[c, :, cols]) * (1.0 - muon_rate * weight_decay)
                - muon_rate * muon_scale * wide(ortho)
            ).astype(jnp.bfloat16)
            return carry

        lax.fori_loop(0, weight.shape[2] // TILE, update, 0)
        store(weight.at[c], new_weight_hbm.at[c], 3 + 2 * MATS + c)

    count = [0] * (2 * chains + len(BATCHES))
    for code in ORDER:
        s = count[code]
        count[code] += 1
        if code < chains:
            group_stage(code, s)
        elif code < 2 * chains:
            shard_stage(code - chains, s)
        else:
            solve_stage(code - 2 * chains, s)
    for copy in started.values():
        copy.wait_send()
    for copy in stores:
        copy.wait()


def finish_kernel(
    owners,
    small,
    energy,
    weight_hbm,
    moment_hbm,
    *refs,
):
    adam, outs = refs[:9], refs[9:-3]
    held, load_sem, store_sem = refs[-3:]
    new_weight, new_moment, owner_sums = outs[:3]
    loads, stores = [], []
    for b in range(MATS):
        for slot, src, dst in ((0, weight_hbm, new_weight), (1, moment_hbm, new_moment)):
            spot = held.at[slot, b]
            loads.append(pltpu.make_async_copy(src.at[b], spot, load_sem.at[slot, b]))
            stores.append(pltpu.make_async_copy(spot, dst.at[b], store_sem.at[slot, b]))
    for load in loads:
        load.start()
    shard = lax.axis_index("shard")
    lane = lax.broadcasted_iota(jnp.int32, (1, 128), 1)
    row = jnp.zeros((1, 128), jnp.float32)
    for i in range(MATS):
        slot = owners[i] * HALF_MATS
        for j in range(i):
            slot = slot + jnp.where(owners[j] == owners[i], 1, 0)
        row = row + jnp.where(lane == slot - shard * HALF_MATS, energy[i : i + 1, :], 0.0)
    owner_sums[...] = row[:, 0:HALF_MATS]
    emb_rows = adam[0].shape[0]
    gains = adam[3].shape[1]
    heads = adam[6].shape[1]

    def emb_step(i, carry):
        cols = pl.ds(pl.multiple_of(i * TILE, TILE), TILE)
        results = adamw(
            adam[0][:, cols], wide(small[0:emb_rows, cols]), adam[1][:, cols], adam[2][:, cols]
        )
        for ref, result in zip(outs[3:6], results):
            ref[:, cols] = result
        return carry

    for load, store in zip(loads, stores):
        load.wait()
        store.start()
    lax.fori_loop(0, adam[0].shape[1] // TILE, emb_step, 0)
    extra = wide(small[emb_rows:SMALL_ROWS, 0 : gains + heads])
    for k, cols in ((1, slice(0, gains)), (2, slice(gains, gains + heads))):
        weight, first, second = adam[3 * k : 3 * k + 3]
        results = adamw(weight[...], extra[0:2, cols], first[...], second[...])
        for ref, result in zip(outs[3 + 3 * k : 6 + 3 * k], results):
            ref[...] = result
    for store in stores:
        store.wait()


def linked_device(
    owners,
    mat_weight,
    mat_grad,
    head_block_momentum,
    emb_weight,
    emb_grad,
    emb_first,
    emb_second,
    norm_weight,
    norm_grad,
    norm_first,
    norm_second,
    qk_weight,
    qk_grad,
    qk_first,
    qk_second,
):
    blocks, rows, width = mat_weight.shape
    levels = [width // PIECES >> (level + 1) for level in range(HALVINGS)]
    chains = (blocks + 1) * PIECES
    in_vmem = pl.BlockSpec(memory_space=pltpu.VMEM)
    anywhere = pl.BlockSpec(memory_space=pl.ANY)
    block_shape = (blocks, rows, width)
    new_weight, new_moment, small_sum, energy = pl.pallas_call(
        linked_kernel,
        out_shape=(
            jax.ShapeDtypeStruct(block_shape, jnp.bfloat16),
            jax.ShapeDtypeStruct(block_shape, jnp.bfloat16),
            jax.ShapeDtypeStruct((SMALL_ROWS, width), jnp.bfloat16),
            jax.ShapeDtypeStruct((8, 128), jnp.float32),
        ),
        in_specs=[in_vmem] * 2 + [anywhere] * 4,
        out_specs=(anywhere, anywhere, in_vmem, in_vmem),
        scratch_shapes=[
            pltpu.VMEM(block_shape, jnp.bfloat16),
            pltpu.VMEM(block_shape, jnp.bfloat16),
            pltpu.VMEM(block_shape, jnp.bfloat16),
            pltpu.VMEM((SMALL_ROWS, width), jnp.bfloat16),
            pltpu.VMEM((blocks + 1, rows, width), jnp.bfloat16),
            pltpu.VMEM((blocks, 2 * rows, width), jnp.bfloat16),
            pltpu.VMEM((blocks, HEAD, HEAD), jnp.float32),
            pltpu.VMEM((blocks, HEAD, HEAD), jnp.float32),
            pltpu.VMEM((blocks, HEAD, HEAD), jnp.float32),
            pltpu.VMEM((blocks, rows, HEAD), jnp.bfloat16),
            pltpu.SemaphoreType.DMA((3 + 3 * blocks,)),
            pltpu.SemaphoreType.DMA((chains, SLOTS)),
            pltpu.SemaphoreType.DMA((chains, SLOTS)),
        ]
        + [pltpu.VMEM((chains, rows, part), jnp.bfloat16) for part in levels]
        + [pltpu.VMEM((chains, LINE - 1, rows, levels[-1] // LINE), jnp.bfloat16)]
        + [pltpu.VMEM((chains, rows, part), jnp.bfloat16) for part in levels],
        compiler_params=pltpu.CompilerParams(
            collective_id=0, has_side_effects=True, vmem_limit_bytes=56 * 1024 * 1024
        ),
    )(norm_grad[0], qk_grad[0], mat_grad[0], emb_grad[0], head_block_momentum, mat_weight)
    adam = (
        emb_weight,
        emb_first,
        emb_second,
        norm_weight,
        norm_first,
        norm_second,
        qk_weight,
        qk_first,
        qk_second,
    )
    return pl.pallas_call(
        finish_kernel,
        out_shape=(
            jax.ShapeDtypeStruct(block_shape, jnp.bfloat16),
            jax.ShapeDtypeStruct(block_shape, jnp.bfloat16),
            jax.ShapeDtypeStruct((1, HALF_MATS), jnp.float32),
        )
        + tuple(jax.ShapeDtypeStruct(a.shape, a.dtype) for a in adam),
        in_specs=[pl.BlockSpec(memory_space=pltpu.SMEM), in_vmem, in_vmem]
        + [anywhere] * 2
        + [in_vmem] * 9,
        out_specs=(anywhere, anywhere) + (in_vmem,) * 10,
        scratch_shapes=[
            pltpu.VMEM((2,) + block_shape, jnp.bfloat16),
            pltpu.SemaphoreType.DMA((2, blocks)),
            pltpu.SemaphoreType.DMA((2, blocks)),
        ],
        compiler_params=pltpu.CompilerParams(vmem_limit_bytes=56 * 1024 * 1024),
    )(owners, small_sum, energy, new_weight, new_moment, *adam)


def solution(mesh):
    plan = on_device
    if links_fit(mesh.shape["group"], mesh.shape["shard"]):
        plan = linked_device
    placed = (
        P(),
        P(None, "shard", None),
        P("group", None, "shard", None),
        P(None, "shard", None),
        P("shard", None),
        P("group", "shard", None),
        P("shard", None),
        P("shard", None),
        P(None, "shard"),
        P("group", None, "shard"),
        P(None, "shard"),
        P(None, "shard"),
        P(),
        P("group", None, None),
        P(),
        P(),
    )
    return jax.shard_map(
        plan,
        mesh=mesh,
        in_specs=placed,
        out_specs=(
            P(None, "shard", None),
            P(None, "shard", None),
            P("shard", None),
            P("shard", None),
            P("shard", None),
            P("shard", None),
            P(None, "shard"),
            P(None, "shard"),
            P(None, "shard"),
            P(),
            P(),
            P(),
        ),
        check_vma=False,
    )
```
